32 devices in a mesh: ta: 16 (over z, x, core), pa: 2 (over y).
Axes of the slice: x: 2, y: 2, z: 4, core: 2. Of those that a mesh axis runs over, the one named last changes fastest.
Arguments:
- occupied_orbitals: bfloat16 [4096, 512], P('pa'), may hold values from -3 to 3
- virtual_orbitals: bfloat16 [4096, 1536], P('pa'), may hold values from -2.5 to 2.5
- occupied_gaps: float32 [512], replicated, may hold values from 0.05 to 2
- virtual_gaps: float32 [1536], replicated, may hold values from 0.05 to 2
- tile_columns: int32 [32, 8], replicated, may hold values from 0 to 31, as said below
- probe_vectors: bfloat16 [32, 4096], P(None, 'ta'), may hold values from -0.1875 to 0.1875
Outputs:
- response: float32 [16, 32, 4096], P('ta', None, 'pa')
The draws below stay inside these ranges and needn't reach their ends.
Inputs may be any that keep to these rules, and one draw needn't show every extreme that they name: `tile_columns`: each row block lists 8 different column blocks, and every column block is listed by some row block.
All inputs are finite; a program needn't handle non-finite values.
Results may differ from the reference program's by a relative error of at most 0.00083.
Values may be sent and summed in bfloat16 or wider, within the bound.
No kernel may reach another device: no remote copies, remote signals or barrier semaphores. Data moves between devices by JAX's collectives and lax.ppermute only.
A program may use at most 128 MiB of HBM per device.

```python
import math
import jax
import jax.numpy as jnp
from jax import lax

NPTS = 4096
NO = 512
NV = 1536
BLK = 128
KB = 8
NT = 32
NVEC = 32
NF = 16


def draw_tile_columns(key, part):
    block_total = NPTS // BLK
    first_key, second_key = jax.random.split(key)
    diagonal_order = jax.random.permutation(first_key, block_total).astype(jnp.int32)
    row_keys = jax.random.split(second_key, block_total)
    shifts = jax.vmap(lambda row_key: jax.random.permutation(row_key, block_total - 1))(row_keys)[:, :KB - 1].astype(jnp.int32)
    rows_here = jnp.arange(block_total, dtype=jnp.int32)
    others = diagonal_order[(rows_here[:, None] + 1 + shifts) % block_total]
    return jnp.concatenate([diagonal_order[:, None], others], axis=1).astype(jnp.int32)


def steps_of(stream_key, extent, cuts, low, top_value):
    def one(position, shards_of):
        draws = jax.random.uniform(jax.random.fold_in(jax.random.fold_in(stream_key, 6), position), (shards_of,), jnp.float32, low / len(cuts), top_value / len(cuts))
        return jnp.repeat(jnp.exp(draws), extent[position] // shards_of).reshape((-1,) + (1,) * (len(extent) - position - 1))

    factor_of = one(*cuts[0])
    for cut in cuts[1:]:
        factor_of = factor_of * one(*cut)
    return factor_of


def gaussian(key, dims, width, limit, cuts=(), kind=jnp.bfloat16):
    result = width * jax.random.normal(key, dims, jnp.float32)
    if cuts:
        result = result * steps_of(key, dims, cuts, -0.22, 0.18)
    return jnp.clip(result, -limit, limit).astype(kind)


def setup_inputs(seed: int = 0) -> dict:
    key_list = jax.random.split(jax.random.key(seed), 7)
    occupied_orbitals = gaussian(key_list[0], (NPTS, NO), 0.21, 3.0, ((0, 2),))
    virtual_orbitals = gaussian(key_list[1], (NPTS, NV), 0.16, 2.5, ((0, 2),))
    occupied_gaps = jnp.clip(jnp.exp(jax.random.uniform(key_list[2], (NO,), jnp.float32, math.log(0.05), math.log(2.0))), 0.05, 2.0)
    virtual_gaps = jnp.clip(jnp.exp(jax.random.uniform(key_list[3], (NV,), jnp.float32, math.log(0.05), math.log(2.0))), 0.05, 2.0)
    tile_columns = draw_tile_columns(jax.random.fold_in(key_list[6], 71), 0)
    probe_vectors = gaussian(key_list[5], (NVEC, NPTS), (KB * BLK) ** -0.5, 0.1875, ((1, 16),))
    return {"occupied_orbitals": occupied_orbitals, "virtual_orbitals": virtual_orbitals, "occupied_gaps": occupied_gaps, "virtual_gaps": virtual_gaps, "tile_columns": tile_columns, "probe_vectors": probe_vectors}


def quadrature_grids(count_times, count_freqs):
    low_time = jnp.log(jnp.float32(0.05))
    high_time = jnp.log(jnp.float32(8.0))
    time_place = (jnp.arange(count_times, dtype=jnp.float32) + 0.5) / count_times
    times_grid = jnp.exp(low_time + (high_time - low_time) * time_place)
    weights_grid = times_grid * (high_time - low_time) / count_times
    low_freq = jnp.log(jnp.float32(0.05))
    high_freq = jnp.log(jnp.float32(20.0))
    freq_place = (jnp.arange(count_freqs, dtype=jnp.float32) + 0.5) / count_freqs
    freqs_grid = jnp.exp(low_freq + (high_freq - low_freq) * freq_place)
    cosine_table = 2.0 * weights_grid[None, :] * jnp.cos(freqs_grid[:, None] * times_grid[None, :])
    return times_grid, cosine_table


def reference(occupied_orbitals, virtual_orbitals, occupied_gaps, virtual_gaps, tile_columns, probe_vectors):
    times_grid, cosine_table = quadrature_grids(NT, NF)
    occ_weights = jnp.exp(-times_grid[:, None] * occupied_gaps[None, :])
    virt_weights = jnp.exp(-times_grid[:, None] * virtual_gaps[None, :])
    highest = lax.Precision.HIGHEST

    def row_block(block_index):
        row_occ = lax.dynamic_slice_in_dim(occupied_orbitals, block_index * BLK, BLK, 0).astype(jnp.float32)
        row_virt = lax.dynamic_slice_in_dim(virtual_orbitals, block_index * BLK, BLK, 0).astype(jnp.float32)

        def one_tile(column_block):
            first_point = column_block * BLK
            col_occ = lax.dynamic_slice_in_dim(occupied_orbitals, first_point, BLK, 0).astype(jnp.float32)
            col_virt = lax.dynamic_slice_in_dim(virtual_orbitals, first_point, BLK, 0).astype(jnp.float32)
            scaled_occ = lax.optimization_barrier((col_occ[None] * occ_weights[:, None, :]).astype(jnp.bfloat16)).astype(jnp.float32)
            scaled_virt = lax.optimization_barrier((col_virt[None] * virt_weights[:, None, :]).astype(jnp.bfloat16)).astype(jnp.float32)
            green_occ = jnp.einsum('tci,ri->tcr', scaled_occ, row_occ, precision=highest)
            green_virt = jnp.einsum('tca,ra->tcr', scaled_virt, row_virt, precision=highest)
            polar = lax.optimization_barrier((green_occ * green_virt).astype(jnp.bfloat16)).astype(jnp.float32)
            col_vectors = lax.dynamic_slice_in_dim(probe_vectors, first_point, BLK, 1).astype(jnp.float32)
            return jnp.einsum('vc,tcr->tvr', col_vectors, polar, precision=highest)

        tile_terms = lax.map(one_tile, tile_columns[block_index].astype(jnp.int32))
        return jnp.sum(tile_terms, axis=0)

    block_total = NPTS // BLK
    block_terms = lax.map(row_block, jnp.arange(block_total).astype(jnp.int32))
    time_terms = jnp.transpose(block_terms, (1, 2, 0, 3)).reshape(NT, NVEC, NPTS)
    return jnp.einsum('kt,tvr->kvr', cosine_table, time_terms, precision=highest)
```

```python
import functools

import jax
import jax.numpy as jnp
from jax import lax
from jax.experimental import pallas as pl
from jax.experimental.pallas import tpu as pltpu
from jax.sharding import PartitionSpec as P

BLK = 128
NT = 32
NVEC = 32
VMEM_BYTES = 52 * 2**20
NT_DIMS = (((1,), (1,)), ((), ()))


def quadrature_grids(count_times, count_freqs):
    low_time = jnp.log(jnp.float32(0.05))
    high_time = jnp.log(jnp.float32(8.0))
    time_place = (jnp.arange(count_times, dtype=jnp.float32) + 0.5) / count_times
    times_grid = jnp.exp(low_time + (high_time - low_time) * time_place)
    weights_grid = times_grid * (high_time - low_time) / count_times
    low_freq = jnp.log(jnp.float32(0.05))
    high_freq = jnp.log(jnp.float32(20.0))
    freq_place = (jnp.arange(count_freqs, dtype=jnp.float32) + 0.5) / count_freqs
    freqs_grid = jnp.exp(low_freq + (high_freq - low_freq) * freq_place)
    cosine_table = 2.0 * weights_grid[None, :] * jnp.cos(freqs_grid[:, None] * times_grid[None, :])
    return (times_grid, cosine_table)


def scale_rows(count, times, gaps_occ, gaps_virt, row_occ, row_virt, scaled_occ, scaled_virt):
    def one_time(t, carry):
        place = pl.ds(pl.multiple_of(t * BLK, BLK), BLK)
        minus_time = -times[t]
        for gaps, row, scaled in (
            (gaps_occ, row_occ, scaled_occ),
            (gaps_virt, row_virt, scaled_virt),
        ):
            weights = jnp.exp(minus_time * gaps[...])
            scaled[place, :] = (row[...].astype(jnp.float32) * weights).astype(jnp.bfloat16)
        return carry

    lax.fori_loop(0, count, one_time, 0)


def load_pair(first, second, pair):
    pair[:BLK] = first[...]
    pair[BLK:] = second[...]


def polar_chunk(place, scaled_occ, scaled_virt, pair_occ, pair_virt):
    green_occ = lax.dot_general(
        scaled_occ[place, :], pair_occ[...], NT_DIMS, preferred_element_type=jnp.float32
    )
    green_virt = lax.dot_general(
        scaled_virt[place, :], pair_virt[...], NT_DIMS, preferred_element_type=jnp.float32
    )
    return (green_occ * green_virt).astype(jnp.bfloat16)


def own_kernel(
    chunk, cols, meta, times, gaps_occ, gaps_virt, row_occ, row_virt,
    occ_0, occ_1, virt_0, virt_1, polar, scaled_occ, scaled_virt, pair_occ, pair_virt,
):
    step = pl.program_id(0)
    rows = scaled_occ.shape[0]

    @pl.when(step == 0)
    def _():
        scale_rows(
            rows // BLK, times, gaps_occ, gaps_virt, row_occ, row_virt, scaled_occ, scaled_virt
        )

    @pl.when(2 * step < meta[1])
    def _():
        load_pair(occ_0, occ_1, pair_occ)
        load_pair(virt_0, virt_1, pair_virt)

        def one_chunk(i, carry):
            place = pl.ds(pl.multiple_of(i * chunk, chunk), chunk)
            polar[0, place, :] = polar_chunk(place, scaled_occ, scaled_virt, pair_occ, pair_virt)
            return carry

        lax.fori_loop(0, rows // chunk, one_chunk, 0)


def rest_kernel(
    chunk, max_pairs, cols, points, counts, dests, times, cosine, gaps_occ, gaps_virt,
    row_virt, row_occ, occ_0, occ_1, virt_0, virt_1, polar_own, probes, out,
    scaled_occ, scaled_virt, pair_occ, pair_virt, pair_probe, terms,
):
    step = pl.program_id(0)
    which = step // max_pairs
    pair = step % max_pairs
    rows = scaled_occ.shape[0]
    count_times = rows // BLK
    blocks = terms.shape[0]
    count = counts[which]

    @pl.when(step == 0)
    def _():
        terms[...] = jnp.zeros_like(terms)

    @pl.when((pair == 0) & (which < blocks - 1) & (count > 0))
    def _():
        scale_rows(
            count_times, times, gaps_occ, gaps_virt, row_occ, row_virt, scaled_occ, scaled_virt
        )

    @pl.when(2 * pair < count)
    def _():
        pair_probe[:, :BLK] = probes[points[2 * step]]
        second = probes[points[2 * step + 1]]
        pair_probe[:, BLK:] = jnp.where(2 * pair + 1 < count, second, jnp.zeros_like(second))

        @pl.when(which < blocks - 1)
        def _():
            load_pair(occ_0, occ_1, pair_occ)
            load_pair(virt_0, virt_1, pair_virt)

            def one_chunk(i, carry):
                place = pl.ds(pl.multiple_of(i * chunk, chunk), chunk)
                polar = polar_chunk(place, scaled_occ, scaled_virt, pair_occ, pair_virt)
                terms[which, :, place] += lax.dot_general(
                    pair_probe[...], polar, NT_DIMS, preferred_element_type=jnp.float32
                )
                return carry

            lax.fori_loop(0, rows // chunk, one_chunk, 0)

        @pl.when(which == blocks - 1)
        def _():
            def one_chunk(i, carry):
                place = pl.ds(pl.multiple_of(i * chunk, chunk), chunk)
                terms[which, :, place] += lax.dot_general(
                    pair_probe[...], polar_own[0, place, :], NT_DIMS,
                    preferred_element_type=jnp.float32,
                )
                return carry

            lax.fori_loop(0, rows // chunk, one_chunk, 0)

    @pl.when(step == pl.num_programs(0) - 1)
    def _():
        for block in range(blocks):
            def one_freq(k, carry):
                total = jnp.zeros((NVEC, BLK), jnp.float32)
                for t in range(count_times):
                    total += cosine[k, t] * terms[block, :, t * BLK : (t + 1) * BLK]
                out[k, dests[block]] = total
                return carry

            lax.fori_loop(0, out.shape[0], one_freq, 0)


def gather_kernel(panels, group, meta, order, parts, out):
    here = meta[0]
    blocks = out.shape[2] // BLK
    for slot in range(blocks):
        total = jnp.zeros((NVEC, BLK), jnp.float32)
        for offset in range(1, panels):
            panel = lax.rem(here + offset, panels)
            for member in range(group):
                total += parts[(slot * group + member) * panels + panel]
        out[0, :, slot * BLK : (slot + 1) * BLK] = total
    for slot in range(blocks):
        total = parts[slot * group * panels + here]
        for member in range(1, group):
            total += parts[(slot * group + member) * panels + here]
        place = pl.ds(pl.multiple_of(order[slot] * BLK, BLK), BLK)
        out[0, :, place] += total


def rank_of(cost):
    index = jnp.arange(cost.shape[0], dtype=jnp.int32)
    before = (cost[None, :] < cost[:, None]) | (
        (cost[None, :] == cost[:, None]) & (index[None, :] < index[:, None])
    )
    return jnp.sum(before.astype(jnp.int32), axis=1)


def shards(
    occupied_orbitals, virtual_orbitals, occupied_gaps, virtual_gaps, tile_columns, probe_vectors
):
    count_ta = lax.axis_size("ta")
    panels = lax.axis_size("pa")
    panel_rows, occ_count = occupied_orbitals.shape
    virt_count = virtual_orbitals.shape[1]
    slice_width = probe_vectors.shape[1]
    tiles = tile_columns.shape[1]
    blocks = panel_rows // BLK
    group = count_ta // blocks
    local_times = NT // group
    rows = local_times * BLK
    chunk = min(rows, 1024)
    max_pairs = (tiles + 1) // 2
    here = lax.axis_index("pa")
    slot = lax.axis_index("ta") // group
    first_time = (lax.axis_index("ta") % group) * local_times

    sent = jnp.concatenate(
        [
            lax.dynamic_slice_in_dim(virtual_orbitals, slot * BLK, BLK, 0),
            lax.dynamic_slice_in_dim(occupied_orbitals, slot * BLK, BLK, 0),
        ],
        axis=1,
    )
    others = [
        lax.ppermute(sent, "pa", [(q, (q - offset) % panels) for q in range(panels)])
        for offset in range(1, panels)
    ]
    other_rows = others[0] if panels == 2 else jnp.concatenate(others, axis=0)

    width = min(slice_width, BLK)
    pieces = probe_vectors.reshape(NVEC, slice_width // width, width).transpose(1, 0, 2)
    spread = jnp.broadcast_to(pieces[None], (count_ta,) + pieces.shape)
    probes = lax.all_to_all(spread, "ta", 0, 0, tiled=True)
    probes = probes.reshape(-1, BLK // width, NVEC, width)
    probes = probes.transpose(0, 2, 1, 3).reshape(-1, NVEC, BLK)

    times_grid, cosine_table = quadrature_grids(NT, count_ta)
    times = lax.dynamic_slice_in_dim(times_grid, first_time, local_times, 0)
    cosine = lax.dynamic_slice_in_dim(cosine_table, first_time, local_times, 1)

    inside = (tile_columns // blocks == here).astype(jnp.int32)
    counts = jnp.sum(inside, axis=1)
    earlier = jnp.arange(tiles)[:, None] < jnp.arange(tiles)[None, :]
    position = jnp.sum(inside[:, :, None] * earlier[None], axis=1)
    chosen = inside[:, :, None] * (position[:, :, None] == jnp.arange(2 * max_pairs)).astype(
        jnp.int32
    )
    listed = jnp.sum(chosen * (tile_columns - here * blocks)[:, :, None], axis=1)

    pairs = (counts + 1) // 2
    cost = (pairs * (2 * tiles) + counts).reshape(panels, blocks)
    own_cost = lax.dynamic_index_in_dim(cost, here, 0, keepdims=False)
    own_rank = rank_of(own_cost)
    other_rank = rank_of(-(jnp.sum(cost, axis=0) - own_cost))
    matches = other_rank[:, None] == own_rank[None, :]
    order = jnp.sum(matches * jnp.arange(blocks, dtype=jnp.int32)[None, :], axis=1)
    order = order.astype(jnp.int32)
    own = order[slot]

    panel_ids = [lax.rem(here + offset, panels) for offset in range(1, panels)] + [here]
    block_ids = [panel * blocks + slot for panel in panel_ids[:-1]] + [here * blocks + own]
    chosen_ids = jnp.stack(block_ids)
    step_counts = counts[chosen_ids]
    step_cols = listed[chosen_ids].reshape(-1)
    dests = jnp.stack(panel_ids).astype(jnp.int32)
    points = step_cols + here * blocks
    own_count = step_counts[panels - 1]
    meta = jnp.stack([own, own_count]).astype(jnp.int32)
    gaps_occ = occupied_gaps.reshape(1, occ_count)
    gaps_virt = virtual_gaps.reshape(1, virt_count)

    smem = pl.BlockSpec(memory_space=pltpu.SMEM)
    whole = lambda shape: pl.BlockSpec(shape, lambda *_: (0,) * len(shape))
    scratch = [
        pltpu.VMEM((rows, occ_count), jnp.bfloat16),
        pltpu.VMEM((rows, virt_count), jnp.bfloat16),
        pltpu.VMEM((2 * BLK, occ_count), jnp.bfloat16),
        pltpu.VMEM((2 * BLK, virt_count), jnp.bfloat16),
    ]

    def own_column(half):
        def place(step, cols, meta):
            last = jnp.maximum((meta[1] + 1) // 2 - 1, 0)
            return (cols[2 * jnp.minimum(step, last) + half], 0)

        return place

    pair_flops = 2 * rows * 2 * BLK * (occ_count + virt_count)
    polar_own = pl.pallas_call(
        functools.partial(own_kernel, chunk),
        grid_spec=pltpu.PrefetchScalarGridSpec(
            num_scalar_prefetch=2,
            grid=(max_pairs,),
            in_specs=[
                smem,
                whole((1, occ_count)),
                whole((1, virt_count)),
                pl.BlockSpec((BLK, occ_count), lambda step, cols, meta: (meta[0], 0)),
                pl.BlockSpec((BLK, virt_count), lambda step, cols, meta: (meta[0], 0)),
                pl.BlockSpec((BLK, occ_count), own_column(0)),
                pl.BlockSpec((BLK, occ_count), own_column(1)),
                pl.BlockSpec((BLK, virt_count), own_column(0)),
                pl.BlockSpec((BLK, virt_count), own_column(1)),
            ],
            out_specs=pl.BlockSpec(
                (1, rows, 2 * BLK),
                lambda step, cols, meta: (
                    jnp.minimum(step, jnp.maximum((meta[1] + 1) // 2 - 1, 0)), 0, 0
                ),
            ),
            scratch_shapes=scratch,
        ),
        out_shape=jax.ShapeDtypeStruct((max_pairs, rows, 2 * BLK), jnp.bfloat16),
        compiler_params=pltpu.CompilerParams(vmem_limit_bytes=VMEM_BYTES),
        cost_estimate=pl.CostEstimate(
            flops=2 * pair_flops, bytes_accessed=2**23, transcendentals=0
        ),
        name="own_tiles",
    )(
        step_cols[-2 * max_pairs :], meta, times, gaps_occ, gaps_virt,
        occupied_orbitals, virtual_orbitals,
        occupied_orbitals, occupied_orbitals, virtual_orbitals, virtual_orbitals,
    )

    def other_column(half):
        def place(step, cols, points, counts, dests):
            which = jnp.minimum(step // max_pairs, panels - 2)
            pair = jnp.where(step // max_pairs > which, max_pairs - 1, step % max_pairs)
            last = jnp.maximum((counts[which] + 1) // 2 - 1, 0)
            return (cols[2 * (which * max_pairs + jnp.minimum(pair, last)) + half], 0)

        return place

    def own_pair(step, cols, points, counts, dests):
        last = jnp.maximum((counts[panels - 1] + 1) // 2 - 1, 0)
        return (jnp.clip(step - max_pairs * (panels - 1), 0, last), 0, 0)

    other = lambda step: jnp.minimum(step // max_pairs, panels - 2)
    partial_response = pl.pallas_call(
        functools.partial(rest_kernel, chunk, max_pairs),
        grid_spec=pltpu.PrefetchScalarGridSpec(
            num_scalar_prefetch=4,
            grid=(panels * max_pairs,),
            in_specs=[
                smem,
                smem,
                whole((1, occ_count)),
                whole((1, virt_count)),
                pl.BlockSpec((BLK, virt_count), lambda step, *_: (other(step), 0)),
                pl.BlockSpec(
                    (BLK, occ_count), lambda step, *_: (other(step), virt_count // occ_count)
                ),
                pl.BlockSpec((BLK, occ_count), other_column(0)),
                pl.BlockSpec((BLK, occ_count), other_column(1)),
                pl.BlockSpec((BLK, virt_count), other_column(0)),
                pl.BlockSpec((BLK, virt_count), other_column(1)),
                pl.BlockSpec((1, rows, 2 * BLK), own_pair),
                whole(probes.shape),
            ],
            out_specs=whole((count_ta, panels, NVEC, BLK)),
            scratch_shapes=scratch
            + [
                pltpu.VMEM((NVEC, 2 * BLK), jnp.bfloat16),
                pltpu.VMEM((panels, NVEC, rows), jnp.float32),
            ],
        ),
        out_shape=jax.ShapeDtypeStruct((count_ta, panels, NVEC, BLK), jnp.float32),
        compiler_params=pltpu.CompilerParams(vmem_limit_bytes=VMEM_BYTES),
        cost_estimate=pl.CostEstimate(
            flops=2 * pair_flops, bytes_accessed=2**23, transcendentals=0
        ),
        name="other_tiles",
    )(
        step_cols, points, step_counts, dests, times, cosine, gaps_occ, gaps_virt,
        other_rows, other_rows,
        occupied_orbitals, occupied_orbitals, virtual_orbitals, virtual_orbitals,
        polar_own, probes,
    )

    parts = lax.all_to_all(
        partial_response.reshape(count_ta * panels, NVEC, BLK), ("ta", "pa"), 0, 0, tiled=True
    )
    return pl.pallas_call(
        functools.partial(gather_kernel, panels, group),
        in_specs=[smem, smem, pl.BlockSpec(memory_space=pltpu.VMEM)],
        out_specs=pl.BlockSpec(memory_space=pltpu.VMEM),
        out_shape=jax.ShapeDtypeStruct((1, NVEC, panel_rows), jnp.float32),
        compiler_params=pltpu.CompilerParams(vmem_limit_bytes=VMEM_BYTES),
        name="sum_parts",
    )(here.reshape(1), order, parts)


def solution(mesh):
    placed = (P("pa", None), P("pa", None), P(), P(), P(), P(None, "ta"))
    return jax.shard_map(
        shards, mesh=mesh, in_specs=placed, out_specs=P("ta", None, "pa"), check_vma=False
    )
```

```python
import functools

import jax
import jax.numpy as jnp
from jax import lax
from jax.experimental import pallas as pl
from jax.experimental.pallas import tpu as pltpu
from jax.sharding import PartitionSpec as P

BLK = 128
NT = 32
NVEC = 32
VMEM_BYTES = 52 * 2**20
NT_DIMS = (((1,), (1,)), ((), ()))
ANY = pl.BlockSpec(memory_space=pl.ANY)
SMEM = pl.BlockSpec(memory_space=pltpu.SMEM)
VMEM = pl.BlockSpec(memory_space=pltpu.VMEM)


def quadrature_grids(count_times, count_freqs):
    low_time = jnp.log(jnp.float32(0.05))
    high_time = jnp.log(jnp.float32(8.0))
    time_place = (jnp.arange(count_times, dtype=jnp.float32) + 0.5) / count_times
    times_grid = jnp.exp(low_time + (high_time - low_time) * time_place)
    weights_grid = times_grid * (high_time - low_time) / count_times
    low_freq = jnp.log(jnp.float32(0.05))
    high_freq = jnp.log(jnp.float32(20.0))
    freq_place = (jnp.arange(count_freqs, dtype=jnp.float32) + 0.5) / count_freqs
    freqs_grid = jnp.exp(low_freq + (high_freq - low_freq) * freq_place)
    cosine_table = 2.0 * weights_grid[None, :] * jnp.cos(freqs_grid[:, None] * times_grid[None, :])
    return (times_grid, cosine_table)


class Plan:
    def __init__(self, panels, tiles, blocks):
        self.panels = panels
        self.tiles = tiles
        self.blocks = blocks
        self.cols = panels
        self.order = panels + panels * tiles
        self.size = self.order + blocks


def prep_kernel(plan, group, tiles_ref, probe, occ, virt, out, sent, spread, costs, ranked, sems):
    panels, tiles, blocks = plan.panels, plan.tiles, plan.blocks
    here = lax.axis_index("pa")
    slot = lax.div(lax.axis_index("ta"), jnp.int32(group))
    virt_count = virt.shape[1]
    place = pl.ds(pl.multiple_of(slot * BLK, BLK), BLK)
    copy_virt = pltpu.make_async_copy(
        virt.at[place, :], sent.at[:, pl.ds(0, virt_count)], sems.at[0]
    )
    copy_occ = pltpu.make_async_copy(
        occ.at[place, :], sent.at[:, pl.ds(virt_count, occ.shape[1])], sems.at[1]
    )
    copy_virt.start()
    copy_occ.start()

    width = spread.shape[3]
    for piece in range(spread.shape[1]):
        value = probe[:, piece * width : (piece + 1) * width]
        for target in range(spread.shape[0]):
            spread[target, piece] = value

    low = here * blocks

    def inside(row, k):
        column = tiles_ref[row, k]
        return ((column >= low) & (column < low + blocks)).astype(jnp.int32)

    def count(row):
        total = jnp.int32(0)
        for k in range(tiles):
            total += inside(row, k)
        return total

    def one_cost(s, carry):
        costs[s] = count(low + s)
        total = jnp.int32(0)
        for offset in range(1, panels):
            total += count(lax.rem(here + offset, panels) * blocks + s)
        costs[blocks + s] = total
        return carry

    lax.fori_loop(0, blocks, one_cost, 0)

    def rank_own(s, carry):
        mine = costs[s]
        rank = jnp.int32(0)
        for j in range(blocks):
            other = costs[j]
            rank += ((other < mine) | ((other == mine) & (j < s))).astype(jnp.int32)
        ranked[rank] = s
        return carry

    lax.fori_loop(0, blocks, rank_own, 0)

    def rank_other(s, carry):
        mine = costs[blocks + s]
        rank = jnp.int32(0)
        for j in range(blocks):
            other = costs[blocks + j]
            rank += ((other > mine) | ((other == mine) & (j < s))).astype(jnp.int32)
        out[plan.order + s] = ranked[rank]
        return carry

    lax.fori_loop(0, blocks, rank_other, 0)

    for which in range(panels):
        if which < panels - 1:
            row = lax.rem(here + which + 1, panels) * blocks + slot
        else:
            row = low + out[plan.order + slot]
        total = jnp.int32(0)
        for k in range(tiles):
            out[plan.cols + which * tiles + total] = tiles_ref[row, k] - low
            total += inside(row, k)
        out[which] = total

    copy_virt.wait()
    copy_occ.wait()


def scale_rows(times, gaps_occ, gaps_virt, row_occ, row_virt, scaled_occ, scaled_virt):
    def one_time(t, carry):
        place = pl.ds(pl.multiple_of(t * BLK, BLK), BLK)
        minus_time = -times[t]
        for gaps, row, scaled in (
            (gaps_occ, row_occ, scaled_occ),
            (gaps_virt, row_virt, scaled_virt),
        ):
            weights = jnp.exp(minus_time * gaps[...].reshape(1, -1))
            scaled[place, :] = (row[...].astype(jnp.float32) * weights).astype(jnp.bfloat16)
        return carry

    lax.fori_loop(0, scaled_occ.shape[0] // BLK, one_time, 0)


def loaded_tiles(count):
    return jnp.where(count == 1, 2, count)


def tile_copies(plan, table, which, tile, occ, virt, cols_occ, cols_virt, sems):
    last = jnp.maximum(table[which] - 1, 0)
    column = table[plan.cols + which * plan.tiles + jnp.minimum(tile, last)]
    source = pl.ds(pl.multiple_of(column * BLK, BLK), BLK)
    target = pl.ds(pl.multiple_of(tile * BLK, BLK), BLK)
    return (
        pltpu.make_async_copy(occ.at[source, :], cols_occ.at[target, :], sems.at[0, tile]),
        pltpu.make_async_copy(virt.at[source, :], cols_virt.at[target, :], sems.at[1, tile]),
    )


def over_groups(count, one_group):
    triple = (lax.rem(count, 2) == 1) & (count >= 3)
    pairs = lax.div(loaded_tiles(count), 2) - triple.astype(jnp.int32)

    def one_pair(g, carry):
        one_group(2 * g, 2)
        return carry

    lax.fori_loop(0, pairs, one_pair, 0)

    @pl.when(triple)
    def _():
        one_group(2 * pairs, 3)


def polar_chunk(columns, place, scaled_occ, scaled_virt, cols_occ, cols_virt):
    green_occ = lax.dot_general(
        cols_occ[columns, :], scaled_occ[place, :], NT_DIMS, preferred_element_type=jnp.float32
    )
    green_virt = lax.dot_general(
        cols_virt[columns, :], scaled_virt[place, :], NT_DIMS, preferred_element_type=jnp.float32
    )
    return (green_occ * green_virt).astype(jnp.bfloat16)


def start_tiles(copies, count):
    def one_tile(tile, carry):
        for copy in copies(tile):
            copy.start()
        return carry

    lax.fori_loop(0, loaded_tiles(count), one_tile, 0)


def own_kernel(
    plan, chunk, table, times, gaps_occ, gaps_virt, occ, virt, polar,
    row_occ, row_virt, scaled_occ, scaled_virt, cols_occ, cols_virt, kept,
    row_sems, tile_sems, out_sems,
):
    which = plan.panels - 1
    slot = lax.div(lax.axis_index("ta"), jnp.int32(lax.axis_size("ta") // plan.blocks))
    own = table[plan.order + slot]
    count = table[which]
    rows = scaled_occ.shape[0]
    place = pl.ds(pl.multiple_of(own * BLK, BLK), BLK)
    row_copies = (
        pltpu.make_async_copy(occ.at[place, :], row_occ, row_sems.at[0]),
        pltpu.make_async_copy(virt.at[place, :], row_virt, row_sems.at[1]),
    )
    copies = lambda tile: tile_copies(
        plan, table, which, tile, occ, virt, cols_occ, cols_virt, tile_sems
    )
    for copy in row_copies:
        copy.start()
    start_tiles(copies, count)
    for copy in row_copies:
        copy.wait()
    scale_rows(times, gaps_occ, gaps_virt, row_occ, row_virt, scaled_occ, scaled_virt)

    def saved(first, size, i):
        columns = pl.ds(pl.multiple_of(first * BLK, BLK), size * BLK)
        part = pl.ds(pl.multiple_of(i * chunk, chunk), chunk)
        return pltpu.make_async_copy(
            kept.at[columns, part], polar.at[columns, part], out_sems.at[first, i]
        )

    def compute(first, size):
        for tile in range(size):
            for copy in copies(first + tile):
                copy.wait()
        columns = pl.ds(pl.multiple_of(first * BLK, BLK), size * BLK)

        def one_chunk(i, carry):
            part = pl.ds(pl.multiple_of(i * chunk, chunk), chunk)
            kept[columns, part] = polar_chunk(
                columns, part, scaled_occ, scaled_virt, cols_occ, cols_virt
            )
            saved(first, size, i).start()
            return carry

        lax.fori_loop(0, rows // chunk, one_chunk, 0)

    def finish(first, size):
        def one_chunk(i, carry):
            saved(first, size, i).wait()
            return carry

        lax.fori_loop(0, rows // chunk, one_chunk, 0)

    over_groups(count, compute)
    over_groups(count, finish)


def rest_kernel(
    plan, chunk, table, times, cosine, gaps_occ, gaps_virt, other_rows, occ, virt, polar, probes,
    out, row_occ, row_virt, scaled_occ, scaled_virt, cols_occ, cols_virt, kept, terms,
    probe_two, probe_three, row_sems, tile_sems, kept_sems,
):
    panels = plan.panels
    here = lax.axis_index("pa")
    rows = scaled_occ.shape[0]
    virt_count = virt.shape[1]
    own_count = table[panels - 1]

    def kept_copies(tile):
        place = pl.ds(pl.multiple_of(tile * BLK, BLK), BLK)
        return (
            pltpu.make_async_copy(polar.at[place, :], kept.at[place, :], kept_sems.at[tile]),
        )

    def load_probes(which, first, size):
        held = probe_two if size == 2 else probe_three
        count = table[which]
        for tile in range(size):
            at = jnp.minimum(first + tile, jnp.maximum(count - 1, 0))
            value = probes[here * plan.blocks + table[plan.cols + which * plan.tiles + at]]
            held[:, tile * BLK : (tile + 1) * BLK] = jnp.where(
                first + tile < count, value, jnp.zeros_like(value)
            )
        return held

    terms[...] = jnp.zeros_like(terms)

    def one_other(which, carry):
        count = table[which]
        place = pl.ds(pl.multiple_of(which * BLK, BLK), BLK)
        row_copies = (
            pltpu.make_async_copy(
                other_rows.at[place, pl.ds(0, virt_count)], row_virt, row_sems.at[0]
            ),
            pltpu.make_async_copy(
                other_rows.at[place, pl.ds(virt_count, occ.shape[1])], row_occ, row_sems.at[1]
            ),
        )
        copies = lambda tile: tile_copies(
            plan, table, which, tile, occ, virt, cols_occ, cols_virt, tile_sems
        )
        for copy in row_copies:
            copy.start()
        start_tiles(copies, count)

        @pl.when(which == 0)
        def _():
            start_tiles(kept_copies, own_count)

        for copy in row_copies:
            copy.wait()
        scale_rows(times, gaps_occ, gaps_virt, row_occ, row_virt, scaled_occ, scaled_virt)

        def compute(first, size):
            for tile in range(size):
                for copy in copies(first + tile):
                    copy.wait()
            held = load_probes(which, first, size)
            columns = pl.ds(pl.multiple_of(first * BLK, BLK), size * BLK)

            def one_chunk(i, carry):
                part = pl.ds(pl.multiple_of(i * chunk, chunk), chunk)
                value = polar_chunk(columns, part, scaled_occ, scaled_virt, cols_occ, cols_virt)
                terms[which, :, part] += jnp.dot(
                    held[...], value, preferred_element_type=jnp.float32
                )
                return carry

            lax.fori_loop(0, rows // chunk, one_chunk, 0)

        over_groups(count, compute)
        return carry

    lax.fori_loop(0, panels - 1, one_other, 0)

    def apply_own(first, size):
        for tile in range(size):
            for copy in kept_copies(first + tile):
                copy.wait()
        held = load_probes(panels - 1, first, size)
        columns = pl.ds(pl.multiple_of(first * BLK, BLK), size * BLK)

        def one_chunk(i, carry):
            part = pl.ds(pl.multiple_of(i * chunk, chunk), chunk)
            terms[panels - 1, :, part] += jnp.dot(
                held[...], kept[columns, part], preferred_element_type=jnp.float32
            )
            return carry

        lax.fori_loop(0, rows // chunk, one_chunk, 0)

    over_groups(own_count, apply_own)

    for which in range(panels):
        dest = lax.rem(here + which + 1, panels)

        def one_freq(k, carry):
            total = jnp.zeros((NVEC, BLK), jnp.float32)
            for t in range(rows // BLK):
                total += cosine[k, t] * terms[which, :, t * BLK : (t + 1) * BLK]
            out[k * panels + dest] = total
            return carry

        lax.fori_loop(0, out.shape[0] // panels, one_freq, 0)


def sum_kernel(plan, group, table, parts, out):
    panels, blocks = plan.panels, plan.blocks
    here = lax.axis_index("pa")
    for slot in range(blocks):
        total = jnp.zeros((NVEC, BLK), jnp.float32)
        for offset in range(1, panels):
            panel = lax.rem(here + offset, panels)
            for member in range(group):
                total += parts[(slot * group + member) * panels + panel]
        out[0, :, slot * BLK : (slot + 1) * BLK] = total
    for slot in range(blocks):
        total = parts[slot * group * panels + here]
        for member in range(1, group):
            total += parts[(slot * group + member) * panels + here]
        place = pl.ds(pl.multiple_of(table[plan.order + slot] * BLK, BLK), BLK)
        out[0, :, place] += total


def shards(
    occupied_orbitals, virtual_orbitals, occupied_gaps, virtual_gaps, tile_columns, probe_vectors
):
    count_ta = lax.axis_size("ta")
    panels = lax.axis_size("pa")
    panel_rows, occ_count = occupied_orbitals.shape
    virt_count = virtual_orbitals.shape[1]
    slice_width = probe_vectors.shape[1]
    tiles = tile_columns.shape[1]
    blocks = panel_rows // BLK
    group = count_ta // blocks
    local_times = NT // group
    rows = local_times * BLK
    chunk = min(rows, 1024)
    chunks = rows // chunk
    plan = Plan(panels, tiles, blocks)
    width = min(slice_width, BLK)
    params = pltpu.CompilerParams(vmem_limit_bytes=VMEM_BYTES)

    table, sent, spread = pl.pallas_call(
        functools.partial(prep_kernel, plan, group),
        in_specs=[SMEM, VMEM, ANY, ANY],
        out_specs=(SMEM, ANY, VMEM),
        out_shape=(
            jax.ShapeDtypeStruct((plan.size,), jnp.int32),
            jax.ShapeDtypeStruct((BLK, virt_count + occ_count), jnp.bfloat16),
            jax.ShapeDtypeStruct((count_ta, slice_width // width, NVEC, width), jnp.bfloat16),
        ),
        scratch_shapes=[
            pltpu.SMEM((2 * blocks,), jnp.int32),
            pltpu.SMEM((blocks,), jnp.int32),
            pltpu.SemaphoreType.DMA((2,)),
        ],
        compiler_params=params,
        name="prep",
    )(tile_columns, probe_vectors, occupied_orbitals, virtual_orbitals)

    others = [
        lax.ppermute(sent, "pa", [(q, (q - offset) % panels) for q in range(panels)])
        for offset in range(1, panels)
    ]
    other_rows = others[0] if panels == 2 else jnp.concatenate(others, axis=0)

    probes = lax.all_to_all(spread, "ta", 0, 0, tiled=True)
    if width < BLK:
        probes = probes.reshape(-1, BLK // width, NVEC, width).transpose(0, 2, 1, 3)
    probes = probes.reshape(-1, NVEC, BLK)

    times, cosine = quadrature_grids(NT, count_ta)
    if group > 1:
        first_time = (lax.axis_index("ta") % group) * local_times
        times = lax.dynamic_slice_in_dim(times, first_time, local_times, 0)
        cosine = lax.dynamic_slice_in_dim(cosine, first_time, local_times, 1)

    scratch = [
        pltpu.VMEM((BLK, occ_count), jnp.bfloat16),
        pltpu.VMEM((BLK, virt_count), jnp.bfloat16),
        pltpu.VMEM((rows, occ_count), jnp.bfloat16),
        pltpu.VMEM((rows, virt_count), jnp.bfloat16),
        pltpu.VMEM((tiles * BLK, occ_count), jnp.bfloat16),
        pltpu.VMEM((tiles * BLK, virt_count), jnp.bfloat16),
        pltpu.VMEM((tiles * BLK, rows), jnp.bfloat16),
    ]
    sems = [pltpu.SemaphoreType.DMA((2,)), pltpu.SemaphoreType.DMA((2, tiles))]
    cost = pl.CostEstimate(
        flops=tiles * BLK * rows * (occ_count + virt_count), bytes_accessed=2**23, transcendentals=0
    )
    polar = pl.pallas_call(
        functools.partial(own_kernel, plan, chunk),
        in_specs=[SMEM, SMEM, VMEM, VMEM, ANY, ANY],
        out_specs=ANY,
        out_shape=jax.ShapeDtypeStruct((tiles * BLK, rows), jnp.bfloat16),
        scratch_shapes=scratch + sems + [pltpu.SemaphoreType.DMA((tiles, chunks))],
        compiler_params=params,
        cost_estimate=cost,
        name="own_tiles",
    )(table, times, occupied_gaps, virtual_gaps, occupied_orbitals, virtual_orbitals)

    partial_response = pl.pallas_call(
        functools.partial(rest_kernel, plan, chunk),
        in_specs=[SMEM, SMEM, SMEM, VMEM, VMEM, ANY, ANY, ANY, ANY, VMEM],
        out_specs=VMEM,
        out_shape=jax.ShapeDtypeStruct((count_ta * panels, NVEC, BLK), jnp.float32),
        scratch_shapes=scratch
        + [
            pltpu.VMEM((panels, NVEC, rows), jnp.float32),
            pltpu.VMEM((NVEC, 2 * BLK), jnp.bfloat16),
            pltpu.VMEM((NVEC, 3 * BLK), jnp.bfloat16),
        ]
        + sems
        + [pltpu.SemaphoreType.DMA((tiles,))],
        compiler_params=params,
        cost_estimate=cost,
        name="other_tiles",
    )(
        table, times, cosine, occupied_gaps, virtual_gaps, other_rows,
        occupied_orbitals, virtual_orbitals, polar, probes,
    )

    parts = lax.all_to_all(partial_response, ("ta", "pa"), 0, 0, tiled=True)
    return pl.pallas_call(
        functools.partial(sum_kernel, plan, group),
        in_specs=[SMEM, VMEM],
        out_specs=VMEM,
        out_shape=jax.ShapeDtypeStruct((1, NVEC, panel_rows), jnp.float32),
        compiler_params=params,
        name="sum_parts",
    )(table, parts)


def solution(mesh):
    placed = (P("pa", None), P("pa", None), P(), P(), P(), P(None, "ta"))
    return jax.shard_map(
        shards, mesh=mesh, in_specs=placed, out_specs=P("ta", None, "pa"), check_vma=False
    )
```

```python
import functools

import jax
import jax.numpy as jnp
from jax import lax
from jax.experimental import pallas as pl
from jax.experimental.pallas import tpu as pltpu
from jax.sharding import PartitionSpec as P

BLK = 128
NT = 32
NVEC = 32
FREQS = 4
VMEM_BYTES = 52 * 2**20
NT_DIMS = (((1,), (1,)), ((), ()))
ANY = pl.BlockSpec(memory_space=pl.ANY)
SMEM = pl.BlockSpec(memory_space=pltpu.SMEM)
VMEM = pl.BlockSpec(memory_space=pltpu.VMEM)


def quadrature_grids(count_times, count_freqs):
    low_time = jnp.log(jnp.float32(0.05))
    high_time = jnp.log(jnp.float32(8.0))
    time_place = (jnp.arange(count_times, dtype=jnp.float32) + 0.5) / count_times
    times_grid = jnp.exp(low_time + (high_time - low_time) * time_place)
    weights_grid = times_grid * (high_time - low_time) / count_times
    low_freq = jnp.log(jnp.float32(0.05))
    high_freq = jnp.log(jnp.float32(20.0))
    freq_place = (jnp.arange(count_freqs, dtype=jnp.float32) + 0.5) / count_freqs
    freqs_grid = jnp.exp(low_freq + (high_freq - low_freq) * freq_place)
    cosine_table = 2.0 * weights_grid[None, :] * jnp.cos(freqs_grid[:, None] * times_grid[None, :])
    return (times_grid, cosine_table)


class Plan:
    def __init__(self, panels, tiles, blocks):
        self.panels = panels
        self.tiles = tiles
        self.blocks = blocks
        self.cols = panels
        self.order = panels + panels * tiles
        self.size = self.order + blocks


def pack_kernel(group, occ, virt, sent, sems):
    slot = lax.div(lax.axis_index("ta"), jnp.int32(group))
    virt_count = virt.shape[1]
    place = pl.ds(pl.multiple_of(slot * BLK, BLK), BLK)
    copies = (
        pltpu.make_async_copy(virt.at[place, :], sent.at[:, pl.ds(0, virt_count)], sems.at[0]),
        pltpu.make_async_copy(
            occ.at[place, :], sent.at[:, pl.ds(virt_count, occ.shape[1])], sems.at[1]
        ),
    )
    for copy in copies:
        copy.start()
    for copy in copies:
        copy.wait()


def plan_kernel(plan, group, tiles_hbm, probe_hbm, after, out, spread, listed, probe, keys, ranked, sems):
    panels, tiles, blocks = plan.panels, plan.tiles, plan.blocks
    here = lax.axis_index("pa")
    slot = lax.div(lax.axis_index("ta"), jnp.int32(group))
    copy_tiles = pltpu.make_async_copy(tiles_hbm, listed, sems.at[0])
    copy_probe = pltpu.make_async_copy(probe_hbm, probe, sems.at[1])
    copy_tiles.start()
    copy_probe.start()
    copy_tiles.wait()

    low = here * blocks

    def inside(row, k):
        column = listed[row, k]
        return ((column >= low) & (column < low + blocks)).astype(jnp.int32)

    def count(row):
        total = jnp.int32(0)
        for k in range(tiles):
            total += inside(row, k)
        return total

    def one_cost(s, carry):
        total = jnp.int32(0)
        for offset in range(1, panels):
            total += count(lax.rem(here + offset, panels) * blocks + s)
        keys[0, s] = count(low + s) * blocks + s
        keys[1, s] = s - total * blocks
        return carry

    lax.fori_loop(0, blocks, one_cost, 0)

    def one_rank(s, carry):
        own, other = keys[0, s], keys[1, s]
        own_rank = jnp.int32(0)
        other_rank = jnp.int32(0)
        for j in range(blocks):
            own_rank += (keys[0, j] < own).astype(jnp.int32)
            other_rank += (keys[1, j] < other).astype(jnp.int32)
        ranked[0, own_rank] = s
        ranked[1, other_rank] = s
        return carry

    lax.fori_loop(0, blocks, one_rank, 0)
    for rank in range(blocks):
        out[plan.order + ranked[1, rank]] = ranked[0, rank]

    for which in range(panels):
        if which < panels - 1:
            row = lax.rem(here + which + 1, panels) * blocks + slot
        else:
            row = low + out[plan.order + slot]
        total = jnp.int32(0)
        for k in range(tiles):
            out[plan.cols + which * tiles + total] = listed[row, k] - low
            total += inside(row, k)
        out[which] = total

    copy_probe.wait()
    width = spread.shape[3]
    for piece in range(spread.shape[1]):
        value = probe[:, piece * width : (piece + 1) * width]
        for target in range(spread.shape[0]):
            spread[target, piece] = value


def scale_rows(times, gaps_occ, gaps_virt, row_occ, row_virt, scaled_occ, scaled_virt):
    def one_time(t, carry):
        place = pl.ds(pl.multiple_of(t * BLK, BLK), BLK)
        minus_time = -times[t]
        for gaps, row, scaled in (
            (gaps_occ, row_occ, scaled_occ),
            (gaps_virt, row_virt, scaled_virt),
        ):
            weights = jnp.exp(minus_time * gaps[...].reshape(1, -1))
            scaled[place, :] = (row[...].astype(jnp.float32) * weights).astype(jnp.bfloat16)
        return carry

    lax.fori_loop(0, scaled_occ.shape[0] // BLK, one_time, 0)


def loaded_tiles(count):
    return jnp.where(count == 1, 2, count)


def tile_copies(plan, table, which, tile, occ, virt, cols_occ, cols_virt, sems):
    last = jnp.maximum(table[which] - 1, 0)
    column = table[plan.cols + which * plan.tiles + jnp.minimum(tile, last)]
    source = pl.ds(pl.multiple_of(column * BLK, BLK), BLK)
    target = pl.ds(pl.multiple_of(tile * BLK, BLK), BLK)
    return (
        pltpu.make_async_copy(occ.at[source, :], cols_occ.at[target, :], sems.at[0, tile]),
        pltpu.make_async_copy(virt.at[source, :], cols_virt.at[target, :], sems.at[1, tile]),
    )


def over_groups(count, one_group):
    triple = (lax.rem(count, 2) == 1) & (count >= 3)
    pairs = lax.div(loaded_tiles(count), 2) - triple.astype(jnp.int32)

    def one_pair(g, carry):
        one_group(2 * g, 2)
        return carry

    lax.fori_loop(0, pairs, one_pair, 0)

    @pl.when(triple)
    def _():
        one_group(2 * pairs, 3)


def polar_chunk(columns, place, scaled_occ, scaled_virt, cols_occ, cols_virt):
    green_occ = lax.dot_general(
        cols_occ[columns, :], scaled_occ[place, :], NT_DIMS, preferred_element_type=jnp.float32
    )
    green_virt = lax.dot_general(
        cols_virt[columns, :], scaled_virt[place, :], NT_DIMS, preferred_element_type=jnp.float32
    )
    return (green_occ * green_virt).astype(jnp.bfloat16)


def start_tiles(copies, count):
    def one_tile(tile, carry):
        for copy in copies(tile):
            copy.start()
        return carry

    lax.fori_loop(0, loaded_tiles(count), one_tile, 0)


def own_kernel(
    plan, chunk, table, times, gaps_occ, gaps_virt, occ, virt, polar,
    row_occ, row_virt, scaled_occ, scaled_virt, cols_occ, cols_virt, kept,
    row_sems, tile_sems, out_sems,
):
    which = plan.panels - 1
    slot = lax.div(lax.axis_index("ta"), jnp.int32(lax.axis_size("ta") // plan.blocks))
    own = table[plan.order + slot]
    count = table[which]
    rows = scaled_occ.shape[0]
    place = pl.ds(pl.multiple_of(own * BLK, BLK), BLK)
    row_copies = (
        pltpu.make_async_copy(occ.at[place, :], row_occ, row_sems.at[0]),
        pltpu.make_async_copy(virt.at[place, :], row_virt, row_sems.at[1]),
    )
    copies = lambda tile: tile_copies(
        plan, table, which, tile, occ, virt, cols_occ, cols_virt, tile_sems
    )
    for copy in row_copies:
        copy.start()
    start_tiles(copies, count)
    for copy in row_copies:
        copy.wait()
    scale_rows(times, gaps_occ, gaps_virt, row_occ, row_virt, scaled_occ, scaled_virt)

    def saved(first, size, i):
        columns = pl.ds(pl.multiple_of(first * BLK, BLK), size * BLK)
        part = pl.ds(pl.multiple_of(i * chunk, chunk), chunk)
        return pltpu.make_async_copy(
            kept.at[columns, part], polar.at[columns, part], out_sems.at[first, i]
        )

    def compute(first, size):
        for tile in range(size):
            for copy in copies(first + tile):
                copy.wait()
        columns = pl.ds(pl.multiple_of(first * BLK, BLK), size * BLK)

        def one_chunk(i, carry):
            part = pl.ds(pl.multiple_of(i * chunk, chunk), chunk)
            kept[columns, part] = polar_chunk(
                columns, part, scaled_occ, scaled_virt, cols_occ, cols_virt
            )
            saved(first, size, i).start()
            return carry

        lax.fori_loop(0, rows // chunk, one_chunk, 0)

    def finish(first, size):
        def one_chunk(i, carry):
            saved(first, size, i).wait()
            return carry

        lax.fori_loop(0, rows // chunk, one_chunk, 0)

    over_groups(count, compute)
    over_groups(count, finish)


def rest_kernel(
    plan, chunk, table, times, cosine, gaps_occ, gaps_virt, other_rows, occ, virt, polar, probes,
    out, row_occ, row_virt, scaled_occ, scaled_virt, cols_occ, cols_virt, kept, terms,
    probe_two, probe_three, row_sems, tile_sems, kept_sems,
):
    panels = plan.panels
    here = lax.axis_index("pa")
    rows = scaled_occ.shape[0]
    virt_count = virt.shape[1]
    own_count = table[panels - 1]

    def kept_copies(tile):
        place = pl.ds(pl.multiple_of(tile * BLK, BLK), BLK)
        return (
            pltpu.make_async_copy(polar.at[place, :], kept.at[place, :], kept_sems.at[tile]),
        )

    def load_probes(which, first, size):
        held = probe_two if size == 2 else probe_three
        count = table[which]
        for tile in range(size):
            at = jnp.minimum(first + tile, jnp.maximum(count - 1, 0))
            value = probes[here * plan.blocks + table[plan.cols + which * plan.tiles + at]]
            held[:, tile * BLK : (tile + 1) * BLK] = jnp.where(
                first + tile < count, value, jnp.zeros_like(value)
            )
        return held

    terms[...] = jnp.zeros_like(terms)

    def one_other(which, carry):
        count = table[which]
        place = pl.ds(pl.multiple_of(which * BLK, BLK), BLK)
        row_copies = (
            pltpu.make_async_copy(
                other_rows.at[place, pl.ds(0, virt_count)], row_virt, row_sems.at[0]
            ),
            pltpu.make_async_copy(
                other_rows.at[place, pl.ds(virt_count, occ.shape[1])], row_occ, row_sems.at[1]
            ),
        )
        copies = lambda tile: tile_copies(
            plan, table, which, tile, occ, virt, cols_occ, cols_virt, tile_sems
        )
        for copy in row_copies:
            copy.start()
        start_tiles(copies, count)

        @pl.when(which == 0)
        def _():
            start_tiles(kept_copies, own_count)

        for copy in row_copies:
            copy.wait()
        scale_rows(times, gaps_occ, gaps_virt, row_occ, row_virt, scaled_occ, scaled_virt)

        def compute(first, size):
            for tile in range(size):
                for copy in copies(first + tile):
                    copy.wait()
            held = load_probes(which, first, size)
            columns = pl.ds(pl.multiple_of(first * BLK, BLK), size * BLK)

            def one_chunk(i, carry):
                part = pl.ds(pl.multiple_of(i * chunk, chunk), chunk)
                value = polar_chunk(columns, part, scaled_occ, scaled_virt, cols_occ, cols_virt)
                terms[which, :, part] += jnp.dot(
                    held[...], value, preferred_element_type=jnp.float32
                )
                return carry

            lax.fori_loop(0, rows // chunk, one_chunk, 0)

        over_groups(count, compute)
        return carry

    lax.fori_loop(0, panels - 1, one_other, 0)

    def apply_own(first, size):
        for tile in range(size):
            for copy in kept_copies(first + tile):
                copy.wait()
        held = load_probes(panels - 1, first, size)
        columns = pl.ds(pl.multiple_of(first * BLK, BLK), size * BLK)

        def one_chunk(i, carry):
            part = pl.ds(pl.multiple_of(i * chunk, chunk), chunk)
            terms[panels - 1, :, part] += jnp.dot(
                held[...], kept[columns, part], preferred_element_type=jnp.float32
            )
            return carry

        lax.fori_loop(0, rows // chunk, one_chunk, 0)

    over_groups(own_count, apply_own)

    for which in range(panels):
        dest = lax.rem(here + which + 1, panels)

        def some_freqs(g, carry):
            totals = [jnp.zeros((NVEC, BLK), jnp.float32)] * FREQS
            for t in range(rows // BLK):
                value = terms[which, :, t * BLK : (t + 1) * BLK]
                for j in range(FREQS):
                    totals[j] += cosine[g * FREQS + j, t] * value
            for j in range(FREQS):
                out[(g * FREQS + j) * panels + dest] = totals[j]
            return carry

        lax.fori_loop(0, out.shape[0] // (panels * FREQS), some_freqs, 0)


def sum_kernel(plan, group, table, parts, out):
    panels, blocks = plan.panels, plan.blocks
    here = lax.axis_index("pa")
    for slot in range(blocks):
        total = jnp.zeros((NVEC, BLK), jnp.float32)
        for offset in range(1, panels):
            panel = lax.rem(here + offset, panels)
            for member in range(group):
                total += parts[(slot * group + member) * panels + panel]
        out[0, :, slot * BLK : (slot + 1) * BLK] = total
    for slot in range(blocks):
        total = parts[slot * group * panels + here]
        for member in range(1, group):
            total += parts[(slot * group + member) * panels + here]
        place = pl.ds(pl.multiple_of(table[plan.order + slot] * BLK, BLK), BLK)
        out[0, :, place] += total


def shards(
    occupied_orbitals, virtual_orbitals, occupied_gaps, virtual_gaps, tile_columns, probe_vectors
):
    count_ta = lax.axis_size("ta")
    panels = lax.axis_size("pa")
    panel_rows, occ_count = occupied_orbitals.shape
    virt_count = virtual_orbitals.shape[1]
    slice_width = probe_vectors.shape[1]
    tiles = tile_columns.shape[1]
    blocks = panel_rows // BLK
    group = count_ta // blocks
    local_times = NT // group
    rows = local_times * BLK
    chunk = min(rows, 2048)
    chunks = rows // chunk
    plan = Plan(panels, tiles, blocks)
    width = min(slice_width, BLK)
    params = pltpu.CompilerParams(vmem_limit_bytes=VMEM_BYTES)

    sent = pl.pallas_call(
        functools.partial(pack_kernel, group),
        in_specs=[ANY, ANY],
        out_specs=ANY,
        out_shape=jax.ShapeDtypeStruct((BLK, virt_count + occ_count), jnp.bfloat16),
        scratch_shapes=[pltpu.SemaphoreType.DMA((2,))],
        compiler_params=params,
        name="pack",
    )(occupied_orbitals, virtual_orbitals)
    table, spread = pl.pallas_call(
        functools.partial(plan_kernel, plan, group),
        in_specs=[ANY, ANY, ANY],
        out_specs=(SMEM, VMEM),
        out_shape=(
            jax.ShapeDtypeStruct((plan.size,), jnp.int32),
            jax.ShapeDtypeStruct((count_ta, slice_width // width, NVEC, width), jnp.bfloat16),
        ),
        scratch_shapes=[
            pltpu.SMEM(tile_columns.shape, jnp.int32),
            pltpu.VMEM(probe_vectors.shape, jnp.bfloat16),
            pltpu.SMEM((2, blocks), jnp.int32),
            pltpu.SMEM((2, blocks), jnp.int32),
            pltpu.SemaphoreType.DMA((2,)),
        ],
        compiler_params=params,
        name="plan",
    )(tile_columns, probe_vectors, sent)

    others = [
        lax.ppermute(sent, "pa", [(q, (q - offset) % panels) for q in range(panels)])
        for offset in range(1, panels)
    ]
    other_rows = others[0] if panels == 2 else jnp.concatenate(others, axis=0)

    probes = lax.all_to_all(spread, "ta", 0, 0, tiled=True)
    if width < BLK:
        probes = probes.reshape(-1, BLK // width, NVEC, width).transpose(0, 2, 1, 3)
    probes = probes.reshape(-1, NVEC, BLK)

    times, cosine = quadrature_grids(NT, count_ta)
    if group > 1:
        first_time = (lax.axis_index("ta") % group) * local_times
        times = lax.dynamic_slice_in_dim(times, first_time, local_times, 0)
        cosine = lax.dynamic_slice_in_dim(cosine, first_time, local_times, 1)

    scratch = [
        pltpu.VMEM((BLK, occ_count), jnp.bfloat16),
        pltpu.VMEM((BLK, virt_count), jnp.bfloat16),
        pltpu.VMEM((rows, occ_count), jnp.bfloat16),
        pltpu.VMEM((rows, virt_count), jnp.bfloat16),
        pltpu.VMEM((tiles * BLK, occ_count), jnp.bfloat16),
        pltpu.VMEM((tiles * BLK, virt_count), jnp.bfloat16),
        pltpu.VMEM((tiles * BLK, rows), jnp.bfloat16),
    ]
    sems = [pltpu.SemaphoreType.DMA((2,)), pltpu.SemaphoreType.DMA((2, tiles))]
    cost = pl.CostEstimate(
        flops=tiles * BLK * rows * (occ_count + virt_count), bytes_accessed=2**23, transcendentals=0
    )
    polar = pl.pallas_call(
        functools.partial(own_kernel, plan, chunk),
        in_specs=[SMEM, SMEM, VMEM, VMEM, ANY, ANY],
        out_specs=ANY,
        out_shape=jax.ShapeDtypeStruct((tiles * BLK, rows), jnp.bfloat16),
        scratch_shapes=scratch + sems + [pltpu.SemaphoreType.DMA((tiles, chunks))],
        compiler_params=params,
        cost_estimate=cost,
        name="own_tiles",
    )(table, times, occupied_gaps, virtual_gaps, occupied_orbitals, virtual_orbitals)

    partial_response = pl.pallas_call(
        functools.partial(rest_kernel, plan, rows),
        in_specs=[SMEM, SMEM, SMEM, VMEM, VMEM, ANY, ANY, ANY, ANY, VMEM],
        out_specs=VMEM,
        out_shape=jax.ShapeDtypeStruct((count_ta * panels, NVEC, BLK), jnp.float32),
        scratch_shapes=scratch
        + [
            pltpu.VMEM((panels, NVEC, rows), jnp.float32),
            pltpu.VMEM((NVEC, 2 * BLK), jnp.bfloat16),
            pltpu.VMEM((NVEC, 3 * BLK), jnp.bfloat16),
        ]
        + sems
        + [pltpu.SemaphoreType.DMA((tiles,))],
        compiler_params=params,
        cost_estimate=cost,
        name="other_tiles",
    )(
        table, times, cosine, occupied_gaps, virtual_gaps, other_rows,
        occupied_orbitals, virtual_orbitals, polar, probes,
    )

    parts = lax.all_to_all(partial_response, ("ta", "pa"), 0, 0, tiled=True)
    return pl.pallas_call(
        functools.partial(sum_kernel, plan, group),
        in_specs=[SMEM, VMEM],
        out_specs=VMEM,
        out_shape=jax.ShapeDtypeStruct((1, NVEC, panel_rows), jnp.float32),
        compiler_params=params,
        name="sum_parts",
    )(table, parts)


def solution(mesh):
    placed = (P("pa", None), P("pa", None), P(), P(), P(), P(None, "ta"))
    return jax.shard_map(
        shards, mesh=mesh, in_specs=placed, out_specs=P("ta", None, "pa"), check_vma=False
    )
```

```python
import functools

import jax
import jax.numpy as jnp
from jax import lax
from jax.experimental import pallas as pl
from jax.experimental.pallas import tpu as pltpu
from jax.sharding import PartitionSpec as P

BLK = 128
NT = 32
NVEC = 32
FREQS = 4
LARGE = pltpu.CompilerParams(vmem_limit_bytes=52 * 2**20)
SMALL = pltpu.CompilerParams(vmem_limit_bytes=52 * 2**20)
NT_DIMS = (((1,), (1,)), ((), ()))
ANY = pl.BlockSpec(memory_space=pl.ANY)
SMEM = pl.BlockSpec(memory_space=pltpu.SMEM)
VMEM = pl.BlockSpec(memory_space=pltpu.VMEM)


def quadrature_grids(count_times, count_freqs):
    low_time = jnp.log(jnp.float32(0.05))
    high_time = jnp.log(jnp.float32(8.0))
    time_place = (jnp.arange(count_times, dtype=jnp.float32) + 0.5) / count_times
    times_grid = jnp.exp(low_time + (high_time - low_time) * time_place)
    weights_grid = times_grid * (high_time - low_time) / count_times
    low_freq = jnp.log(jnp.float32(0.05))
    high_freq = jnp.log(jnp.float32(20.0))
    freq_place = (jnp.arange(count_freqs, dtype=jnp.float32) + 0.5) / count_freqs
    freqs_grid = jnp.exp(low_freq + (high_freq - low_freq) * freq_place)
    cosine_table = 2.0 * weights_grid[None, :] * jnp.cos(freqs_grid[:, None] * times_grid[None, :])
    return (times_grid, cosine_table)


class Plan:
    def __init__(self, panels, tiles, blocks):
        self.panels = panels
        self.tiles = tiles
        self.blocks = blocks
        self.cols = panels
        self.order = panels + panels * tiles
        self.size = self.order + blocks


def pack_kernel(group, occ, virt, sent, sems):
    slot = lax.div(lax.axis_index("ta"), jnp.int32(group))
    virt_count = virt.shape[1]
    place = pl.ds(pl.multiple_of(slot * BLK, BLK), BLK)
    copies = (
        pltpu.make_async_copy(virt.at[place, :], sent.at[:, pl.ds(0, virt_count)], sems.at[0]),
        pltpu.make_async_copy(
            occ.at[place, :], sent.at[:, pl.ds(virt_count, occ.shape[1])], sems.at[1]
        ),
    )
    for copy in copies:
        copy.start()
    for copy in copies:
        copy.wait()


def plan_kernel(plan, group, tiles_hbm, probe_hbm, after, out, spread, listed, probe, keys, ranked, sems):
    panels, tiles, blocks = plan.panels, plan.tiles, plan.blocks
    here = lax.axis_index("pa")
    slot = lax.div(lax.axis_index("ta"), jnp.int32(group))
    copy_tiles = pltpu.make_async_copy(tiles_hbm, listed, sems.at[0])
    copy_probe = pltpu.make_async_copy(probe_hbm, probe, sems.at[1])
    copy_tiles.start()
    copy_probe.start()
    copy_tiles.wait()

    low = here * blocks

    def inside(row, k):
        column = listed[row, k]
        return ((column >= low) & (column < low + blocks)).astype(jnp.int32)

    def count(row):
        total = jnp.int32(0)
        for k in range(tiles):
            total += inside(row, k)
        return total

    def one_cost(s, carry):
        total = jnp.int32(0)
        for offset in range(1, panels):
            total += count(lax.rem(here + offset, panels) * blocks + s)
        keys[0, s] = count(low + s) * blocks + s
        keys[1, s] = s - total * blocks
        return carry

    lax.fori_loop(0, blocks, one_cost, 0)

    def one_rank(s, carry):
        own, other = keys[0, s], keys[1, s]
        own_rank = jnp.int32(0)
        other_rank = jnp.int32(0)
        for j in range(blocks):
            own_rank += (keys[0, j] < own).astype(jnp.int32)
            other_rank += (keys[1, j] < other).astype(jnp.int32)
        ranked[0, own_rank] = s
        ranked[1, other_rank] = s
        return carry

    lax.fori_loop(0, blocks, one_rank, 0)
    for rank in range(blocks):
        out[plan.order + ranked[1, rank]] = ranked[0, rank]

    for which in range(panels):
        if which < panels - 1:
            row = lax.rem(here + which + 1, panels) * blocks + slot
        else:
            row = low + out[plan.order + slot]
        total = jnp.int32(0)
        for k in range(tiles):
            out[plan.cols + which * tiles + total] = listed[row, k] - low
            total += inside(row, k)
        out[which] = total

    copy_probe.wait()
    width = spread.shape[3]
    for piece in range(spread.shape[1]):
        value = probe[:, piece * width : (piece + 1) * width]
        for target in range(spread.shape[0]):
            spread[target, piece] = value


def scale_part(first_time, times, gaps_occ, gaps_virt, row_occ, row_virt, scaled, unrolled):
    def one_time(u, carry):
        place = pl.ds(u * BLK if unrolled else pl.multiple_of(u * BLK, BLK), BLK)
        minus_time = -times[first_time + u]
        for gaps, row, target in zip((gaps_occ, gaps_virt), (row_occ, row_virt), scaled):
            weights = jnp.exp(minus_time * gaps[...].reshape(1, -1))
            target[place, :] = (row[...].astype(jnp.float32) * weights).astype(jnp.bfloat16)
        return carry

    count = scaled[0].shape[0] // BLK
    if unrolled:
        for u in range(count):
            one_time(u, 0)
    else:
        lax.fori_loop(0, count, one_time, 0)


def starts_of(scaled):
    starts = [0]
    for part in scaled:
        starts.append(starts[-1] + part[0].shape[0])
    return starts


def loaded_tiles(count):
    return jnp.where(count == 1, 2, count)


def tile_copies(plan, table, which, tile, occ, virt, cols_occ, cols_virt, sems):
    last = jnp.maximum(table[which] - 1, 0)
    column = table[plan.cols + which * plan.tiles + jnp.minimum(tile, last)]
    source = pl.ds(pl.multiple_of(column * BLK, BLK), BLK)
    target = pl.ds(pl.multiple_of(tile * BLK, BLK), BLK)
    return (
        pltpu.make_async_copy(occ.at[source, :], cols_occ.at[target, :], sems.at[0, tile]),
        pltpu.make_async_copy(virt.at[source, :], cols_virt.at[target, :], sems.at[1, tile]),
    )


def over_groups(count, begin, later):
    triple = (lax.rem(count, 2) == 1) & (count >= 3)
    begun = jnp.where(triple, 3, 2)

    @pl.when(triple)
    def _():
        begin(0, 3)

    @pl.when((count > 0) & jnp.logical_not(triple))
    def _():
        begin(0, 2)

    def one_pair(g, carry):
        later(begun + 2 * g, 2)
        return carry

    lax.fori_loop(0, lax.div(loaded_tiles(count) - begun, 2), one_pair, 0)


def tile_range(first, size):
    if isinstance(first, int):
        return pl.ds(first * BLK, size * BLK)
    return pl.ds(pl.multiple_of(first * BLK, BLK), size * BLK)


def polar_part(columns, scaled, cols_occ, cols_virt):
    green_occ = lax.dot_general(
        cols_occ[columns, :], scaled[0][...], NT_DIMS, preferred_element_type=jnp.float32
    )
    green_virt = lax.dot_general(
        cols_virt[columns, :], scaled[1][...], NT_DIMS, preferred_element_type=jnp.float32
    )
    return (green_occ * green_virt).astype(jnp.bfloat16)


def over_tiles(count, scale, copies, scaled, cols_occ, cols_virt, open_group):
    starts = starts_of(scaled)

    def one_group(first, size, begins):
        for tile in range(size):
            for copy in copies(first + tile):
                copy.wait()
        take = open_group(first, size)
        if begins:
            scale(0, False)
        for i, part in enumerate(scaled):
            if begins and i + 1 < len(scaled):
                scale(i + 1, True)
            value = polar_part(tile_range(first, size), part, cols_occ, cols_virt)
            take(i, pl.ds(starts[i], starts[i + 1] - starts[i]), value)

    over_groups(
        count,
        lambda first, size: one_group(first, size, True),
        lambda first, size: one_group(first, size, False),
    )


def start_tiles(copies, count):
    def one_tile(tile, carry):
        for copy in copies(tile):
            copy.start()
        return carry

    lax.fori_loop(0, loaded_tiles(count), one_tile, 0)


def wait_tiles(copies, count):
    def one_tile(tile, carry):
        for copy in copies(tile):
            copy.wait()
        return carry

    lax.fori_loop(0, loaded_tiles(count), one_tile, 0)


def own_kernel(
    plan, table, times, gaps_occ, gaps_virt, occ, virt, polar,
    row_occ, row_virt, scaled, cols_occ, cols_virt, kept, row_sems, tile_sems, save_sems,
):
    which = plan.panels - 1
    slot = lax.div(lax.axis_index("ta"), jnp.int32(lax.axis_size("ta") // plan.blocks))
    own = table[plan.order + slot]
    count = table[which]
    place = pl.ds(pl.multiple_of(own * BLK, BLK), BLK)
    row_copies = (
        pltpu.make_async_copy(occ.at[place, :], row_occ, row_sems.at[0]),
        pltpu.make_async_copy(virt.at[place, :], row_virt, row_sems.at[1]),
    )
    copies = lambda tile: tile_copies(
        plan, table, which, tile, occ, virt, cols_occ, cols_virt, tile_sems
    )
    for copy in row_copies:
        copy.start()
    start_tiles(copies, count)
    for copy in row_copies:
        copy.wait()

    def scale(i, unrolled):
        scale_part(
            starts_of(scaled)[i] // BLK, times, gaps_occ, gaps_virt, row_occ, row_virt,
            scaled[i], unrolled,
        )

    starts = starts_of(scaled)

    def saved(first, size, i):
        part = (tile_range(first, size), pl.ds(starts[i], starts[i + 1] - starts[i]))
        return pltpu.make_async_copy(kept.at[part], polar.at[part], save_sems.at[first, i])

    def open_group(first, size):
        def take(i, part, value):
            kept[tile_range(first, size), part] = value
            saved(first, size, i).start()

        return take

    def finish(first, size):
        for i in range(len(scaled)):
            saved(first, size, i).wait()

    over_tiles(count, scale, copies, scaled, cols_occ, cols_virt, open_group)
    over_groups(count, finish, finish)


def rest_kernel(
    plan, table, times, cosine, gaps_occ, gaps_virt, other_rows, occ, virt, polar, probes,
    out, row_occ, row_virt, scaled, cols_occ, cols_virt, kept, fresh, terms,
    probe_two, probe_three, row_sems, tile_sems, kept_sems,
):
    panels = plan.panels
    here = lax.axis_index("pa")
    rows = terms.shape[2]
    virt_count = virt.shape[1]

    def kept_copies(tile):
        place = tile_range(tile, 1)
        return (
            pltpu.make_async_copy(polar.at[place, :], kept.at[place, :], kept_sems.at[tile]),
        )

    def load_probes(which, first, size):
        held = probe_two if size == 2 else probe_three
        count = table[which]
        for tile in range(size):
            at = jnp.minimum(first + tile, jnp.maximum(count - 1, 0))
            value = probes[here * plan.blocks + table[plan.cols + which * plan.tiles + at]]
            held[:, tile * BLK : (tile + 1) * BLK] = jnp.where(
                first + tile < count, value, jnp.zeros_like(value)
            )
        return held

    terms[...] = jnp.zeros_like(terms)

    def apply(which, count, polars):
        def one_group(first, size):
            held = load_probes(which, first, size)
            terms[which] += jnp.dot(
                held[...], polars[tile_range(first, size), :], preferred_element_type=jnp.float32
            )

        over_groups(count, one_group, one_group)

    def one_other(which, carry):
        count = table[which]
        place = pl.ds(pl.multiple_of(which * BLK, BLK), BLK)
        row_copies = (
            pltpu.make_async_copy(
                other_rows.at[place, pl.ds(0, virt_count)], row_virt, row_sems.at[0]
            ),
            pltpu.make_async_copy(
                other_rows.at[place, pl.ds(virt_count, occ.shape[1])], row_occ, row_sems.at[1]
            ),
        )
        copies = lambda tile: tile_copies(
            plan, table, which, tile, occ, virt, cols_occ, cols_virt, tile_sems
        )
        for copy in row_copies:
            copy.start()
        start_tiles(copies, count)

        @pl.when(which == 0)
        def _():
            start_tiles(kept_copies, table[panels - 1])

        for copy in row_copies:
            copy.wait()

        def scale(i, unrolled):
            scale_part(
                starts_of(scaled)[i] // BLK, times, gaps_occ, gaps_virt, row_occ, row_virt,
                scaled[i], unrolled,
            )

        def open_group(first, size):
            def take(i, part, value):
                fresh[tile_range(first, size), part] = value

            return take

        over_tiles(count, scale, copies, scaled, cols_occ, cols_virt, open_group)
        apply(which, count, fresh)
        return carry

    lax.fori_loop(0, panels - 1, one_other, 0)
    wait_tiles(kept_copies, table[panels - 1])
    apply(panels - 1, table[panels - 1], kept)

    for which in range(panels):
        dest = lax.rem(here + which + 1, panels)

        def some_freqs(g, carry):
            totals = [jnp.zeros((NVEC, BLK), jnp.float32)] * FREQS
            for t in range(rows // BLK):
                value = terms[which, :, t * BLK : (t + 1) * BLK]
                for j in range(FREQS):
                    totals[j] += cosine[g * FREQS + j, t] * value
            for j in range(FREQS):
                out[(g * FREQS + j) * panels + dest] = totals[j]
            return carry

        lax.fori_loop(0, out.shape[0] // (panels * FREQS), some_freqs, 0)


def sum_kernel(plan, group, table, parts, out):
    panels, blocks = plan.panels, plan.blocks
    here = lax.axis_index("pa")
    for slot in range(blocks):
        total = jnp.zeros((NVEC, BLK), jnp.float32)
        for offset in range(1, panels):
            panel = lax.rem(here + offset, panels)
            for member in range(group):
                total += parts[(slot * group + member) * panels + panel]
        out[0, :, slot * BLK : (slot + 1) * BLK] = total
    for slot in range(blocks):
        total = parts[slot * group * panels + here]
        for member in range(1, group):
            total += parts[(slot * group + member) * panels + here]
        place = pl.ds(pl.multiple_of(table[plan.order + slot] * BLK, BLK), BLK)
        out[0, :, place] += total


def shards(
    occupied_orbitals, virtual_orbitals, occupied_gaps, virtual_gaps, tile_columns, probe_vectors
):
    count_ta = lax.axis_size("ta")
    panels = lax.axis_size("pa")
    panel_rows, occ_count = occupied_orbitals.shape
    virt_count = virtual_orbitals.shape[1]
    slice_width = probe_vectors.shape[1]
    tiles = tile_columns.shape[1]
    blocks = panel_rows // BLK
    group = count_ta // blocks
    local_times = NT // group
    rows = local_times * BLK
    if local_times % 8:
        parts_rows = (rows,)
    else:
        parts_rows = (rows // 4,) * 4
    plan = Plan(panels, tiles, blocks)
    width = min(slice_width, BLK)

    sent = pl.pallas_call(
        functools.partial(pack_kernel, group),
        in_specs=[ANY, ANY],
        out_specs=ANY,
        out_shape=jax.ShapeDtypeStruct((BLK, virt_count + occ_count), jnp.bfloat16),
        scratch_shapes=[pltpu.SemaphoreType.DMA((2,))],
        compiler_params=SMALL,
        name="pack",
    )(occupied_orbitals, virtual_orbitals)
    table, spread = pl.pallas_call(
        functools.partial(plan_kernel, plan, group),
        in_specs=[ANY, ANY, ANY],
        out_specs=(SMEM, VMEM),
        out_shape=(
            jax.ShapeDtypeStruct((plan.size,), jnp.int32),
            jax.ShapeDtypeStruct((count_ta, slice_width // width, NVEC, width), jnp.bfloat16),
        ),
        scratch_shapes=[
            pltpu.SMEM(tile_columns.shape, jnp.int32),
            pltpu.VMEM(probe_vectors.shape, jnp.bfloat16),
            pltpu.SMEM((2, blocks), jnp.int32),
            pltpu.SMEM((2, blocks), jnp.int32),
            pltpu.SemaphoreType.DMA((2,)),
        ],
        compiler_params=SMALL,
        name="plan",
    )(tile_columns, probe_vectors, sent)

    others = [
        lax.ppermute(sent, "pa", [(q, (q - offset) % panels) for q in range(panels)])
        for offset in range(1, panels)
    ]
    other_rows = others[0] if panels == 2 else jnp.concatenate(others, axis=0)

    probes = lax.all_to_all(spread, "ta", 0, 0, tiled=True)
    if width < BLK:
        probes = probes.reshape(-1, BLK // width, NVEC, width).transpose(0, 2, 1, 3)
    probes = probes.reshape(-1, NVEC, BLK)

    times, cosine = quadrature_grids(NT, count_ta)
    if group > 1:
        first_time = (lax.axis_index("ta") % group) * local_times
        times = lax.dynamic_slice_in_dim(times, first_time, local_times, 0)
        cosine = lax.dynamic_slice_in_dim(cosine, first_time, local_times, 1)

    held_tiles = max(tiles, 2) * BLK
    scratch = [
        pltpu.VMEM((BLK, occ_count), jnp.bfloat16),
        pltpu.VMEM((BLK, virt_count), jnp.bfloat16),
        [
            (
                pltpu.VMEM((part, occ_count), jnp.bfloat16),
                pltpu.VMEM((part, virt_count), jnp.bfloat16),
            )
            for part in parts_rows
        ],
        pltpu.VMEM((held_tiles, occ_count), jnp.bfloat16),
        pltpu.VMEM((held_tiles, virt_count), jnp.bfloat16),
        pltpu.VMEM((held_tiles, rows), jnp.bfloat16),
    ]
    sems = [pltpu.SemaphoreType.DMA((2,)), pltpu.SemaphoreType.DMA((2, max(tiles, 2)))]
    cost = pl.CostEstimate(
        flops=tiles * BLK * rows * (occ_count + virt_count), bytes_accessed=2**23, transcendentals=0
    )
    polar = pl.pallas_call(
        functools.partial(own_kernel, plan),
        in_specs=[SMEM, SMEM, VMEM, VMEM, ANY, ANY],
        out_specs=ANY,
        out_shape=jax.ShapeDtypeStruct((held_tiles, rows), jnp.bfloat16),
        scratch_shapes=scratch
        + sems
        + [pltpu.SemaphoreType.DMA((max(tiles, 2), len(parts_rows)))],
        compiler_params=LARGE,
        cost_estimate=cost,
        name="own_tiles",
    )(table, times, occupied_gaps, virtual_gaps, occupied_orbitals, virtual_orbitals)

    partial_response = pl.pallas_call(
        functools.partial(rest_kernel, plan),
        in_specs=[SMEM, SMEM, SMEM, VMEM, VMEM, ANY, ANY, ANY, ANY, VMEM],
        out_specs=VMEM,
        out_shape=jax.ShapeDtypeStruct((count_ta * panels, NVEC, BLK), jnp.float32),
        scratch_shapes=scratch
        + [
            pltpu.VMEM((held_tiles, rows), jnp.bfloat16),
            pltpu.VMEM((panels, NVEC, rows), jnp.float32),
            pltpu.VMEM((NVEC, 2 * BLK), jnp.bfloat16),
            pltpu.VMEM((NVEC, 3 * BLK), jnp.bfloat16),
        ]
        + sems
        + [pltpu.SemaphoreType.DMA((max(tiles, 2),))],
        compiler_params=LARGE,
        cost_estimate=cost,
        name="other_tiles",
    )(
        table, times, cosine, occupied_gaps, virtual_gaps, other_rows,
        occupied_orbitals, virtual_orbitals, polar, probes,
    )

    parts = lax.all_to_all(partial_response, ("ta", "pa"), 0, 0, tiled=True)
    return pl.pallas_call(
        functools.partial(sum_kernel, plan, group),
        in_specs=[SMEM, VMEM],
        out_specs=VMEM,
        out_shape=jax.ShapeDtypeStruct((1, NVEC, panel_rows), jnp.float32),
        compiler_params=SMALL,
        name="sum_parts",
    )(table, parts)


def solution(mesh):
    placed = (P("pa", None), P("pa", None), P(), P(), P(), P(None, "ta"))
    return jax.shard_map(
        shards, mesh=mesh, in_specs=placed, out_specs=P("ta", None, "pa"), check_vma=False
    )
```

```python
import functools

import jax
import jax.numpy as jnp
from jax import lax
from jax.experimental import pallas as pl
from jax.experimental.pallas import tpu as pltpu
from jax.sharding import PartitionSpec as P

BLK = 128
NT = 32
NVEC = 32
FREQS = 4
LARGE = pltpu.CompilerParams(vmem_limit_bytes=52 * 2**20)
SMALL = pltpu.CompilerParams(vmem_limit_bytes=52 * 2**20)
NT_DIMS = (((1,), (1,)), ((), ()))
ANY = pl.BlockSpec(memory_space=pl.ANY)
SMEM = pl.BlockSpec(memory_space=pltpu.SMEM)
VMEM = pl.BlockSpec(memory_space=pltpu.VMEM)


def quadrature_grids(count_times, count_freqs):
    low_time = jnp.log(jnp.float32(0.05))
    high_time = jnp.log(jnp.float32(8.0))
    time_place = (jnp.arange(count_times, dtype=jnp.float32) + 0.5) / count_times
    times_grid = jnp.exp(low_time + (high_time - low_time) * time_place)
    weights_grid = times_grid * (high_time - low_time) / count_times
    low_freq = jnp.log(jnp.float32(0.05))
    high_freq = jnp.log(jnp.float32(20.0))
    freq_place = (jnp.arange(count_freqs, dtype=jnp.float32) + 0.5) / count_freqs
    freqs_grid = jnp.exp(low_freq + (high_freq - low_freq) * freq_place)
    cosine_table = 2.0 * weights_grid[None, :] * jnp.cos(freqs_grid[:, None] * times_grid[None, :])
    return (times_grid, cosine_table)


class Plan:
    def __init__(self, panels, tiles, blocks):
        self.panels = panels
        self.tiles = tiles
        self.blocks = blocks
        self.cols = panels
        self.order = panels + panels * tiles
        self.size = self.order + blocks


def pack_kernel(group, occ, virt, sent, sems):
    slot = lax.div(lax.axis_index("ta"), jnp.int32(group))
    virt_count = virt.shape[1]
    place = pl.ds(pl.multiple_of(slot * BLK, BLK), BLK)
    copies = (
        pltpu.make_async_copy(virt.at[place, :], sent.at[:, pl.ds(0, virt_count)], sems.at[0]),
        pltpu.make_async_copy(
            occ.at[place, :], sent.at[:, pl.ds(virt_count, occ.shape[1])], sems.at[1]
        ),
    )
    for copy in copies:
        copy.start()
    for copy in copies:
        copy.wait()


def plan_kernel(
    plan, group, tiles_hbm, probe_hbm, after, out, spread,
    listed, probe, keys, places, ranked, sems,
):
    panels, tiles, blocks = plan.panels, plan.tiles, plan.blocks
    here = lax.axis_index("pa")
    slot = lax.div(lax.axis_index("ta"), jnp.int32(group))
    copy_tiles = pltpu.make_async_copy(tiles_hbm, listed, sems.at[0])
    copy_probe = pltpu.make_async_copy(probe_hbm, probe, sems.at[1])
    copy_tiles.start()
    copy_probe.start()
    copy_tiles.wait()

    low = here * blocks

    def inside(row, k):
        column = listed[row, k]
        return ((column >= low) & (column < low + blocks)).astype(jnp.int32)

    def count(row):
        total = jnp.int32(0)
        for k in range(tiles):
            total += inside(row, k)
        return total

    most = max(tiles, tiles * (panels - 1))
    for kind in range(2):
        for value in range(most + 2):
            places[kind, value] = 0

    def one_count(s, carry):
        total = jnp.int32(0)
        for offset in range(1, panels):
            total += count(lax.rem(here + offset, panels) * blocks + s)
        for kind, value in enumerate((count(low + s), most - total)):
            keys[kind, s] = value
            places[kind, value + 1] = places[kind, value + 1] + 1
        return carry

    lax.fori_loop(0, blocks, one_count, 0)
    for kind in range(2):
        first = jnp.int32(0)
        for value in range(1, most + 2):
            first += places[kind, value]
            places[kind, value] = first

    def one_place(s, carry):
        for kind in range(2):
            value = keys[kind, s]
            rank = places[kind, value]
            places[kind, value] = rank + 1
            ranked[kind, rank] = s
        return carry

    lax.fori_loop(0, blocks, one_place, 0)
    for rank in range(blocks):
        out[plan.order + ranked[1, rank]] = ranked[0, rank]

    for which in range(panels):
        if which < panels - 1:
            row = lax.rem(here + which + 1, panels) * blocks + slot
        else:
            row = low + out[plan.order + slot]
        total = jnp.int32(0)
        for k in range(tiles):
            out[plan.cols + which * tiles + total] = listed[row, k] - low
            total += inside(row, k)
        out[which] = total

    copy_probe.wait()
    width = spread.shape[3]
    for piece in range(spread.shape[1]):
        value = probe[:, piece * width : (piece + 1) * width]
        for target in range(spread.shape[0]):
            spread[target, piece] = value


def scale_part(first_time, times, gaps_occ, gaps_virt, row_occ, row_virt, scaled, unrolled):
    def one_time(u, carry):
        place = pl.ds(u * BLK if unrolled else pl.multiple_of(u * BLK, BLK), BLK)
        minus_time = -times[first_time + u]
        for gaps, row, target in zip((gaps_occ, gaps_virt), (row_occ, row_virt), scaled):
            weights = jnp.exp(minus_time * gaps[...].reshape(1, -1))
            target[place, :] = (row[...].astype(jnp.float32) * weights).astype(jnp.bfloat16)
        return carry

    count = scaled[0].shape[0] // BLK
    if unrolled:
        for u in range(count):
            one_time(u, 0)
    else:
        lax.fori_loop(0, count, one_time, 0)


def starts_of(scaled):
    starts = [0]
    for part in scaled:
        starts.append(starts[-1] + part[0].shape[0])
    return starts


def loaded_tiles(count):
    return jnp.where(count == 1, 2, count)


def tile_copies(plan, table, which, tile, occ, virt, cols_occ, cols_virt, sems):
    last = jnp.maximum(table[which] - 1, 0)
    column = table[plan.cols + which * plan.tiles + jnp.minimum(tile, last)]
    source = pl.ds(pl.multiple_of(column * BLK, BLK), BLK)
    target = pl.ds(pl.multiple_of(tile * BLK, BLK), BLK)
    return (
        pltpu.make_async_copy(occ.at[source, :], cols_occ.at[target, :], sems.at[0, tile]),
        pltpu.make_async_copy(virt.at[source, :], cols_virt.at[target, :], sems.at[1, tile]),
    )


def over_groups(count, begin, later):
    triple = (lax.rem(count, 2) == 1) & (count >= 3)
    begun = jnp.where(triple, 3, 2)

    @pl.when(triple)
    def _():
        begin(0, 3)

    @pl.when((count > 0) & jnp.logical_not(triple))
    def _():
        begin(0, 2)

    def one_pair(g, carry):
        later(begun + 2 * g, 2)
        return carry

    lax.fori_loop(0, lax.div(loaded_tiles(count) - begun, 2), one_pair, 0)


def tile_range(first, size):
    if isinstance(first, int):
        return pl.ds(first * BLK, size * BLK)
    return pl.ds(pl.multiple_of(first * BLK, BLK), size * BLK)


def polar_part(columns, scaled, cols_occ, cols_virt):
    green_occ = lax.dot_general(
        cols_occ[columns, :], scaled[0][...], NT_DIMS, preferred_element_type=jnp.float32
    )
    green_virt = lax.dot_general(
        cols_virt[columns, :], scaled[1][...], NT_DIMS, preferred_element_type=jnp.float32
    )
    return (green_occ * green_virt).astype(jnp.bfloat16)


def over_tiles(count, scale, copies, scaled, cols_occ, cols_virt, open_group):
    starts = starts_of(scaled)

    def one_group(first, size, begins):
        for tile in range(size):
            for copy in copies(first + tile):
                copy.wait()
        take = open_group(first, size)
        if begins:
            scale(0, False)
        for i, part in enumerate(scaled):
            if begins and i + 1 < len(scaled):
                scale(i + 1, True)
            value = polar_part(tile_range(first, size), part, cols_occ, cols_virt)
            take(i, pl.ds(starts[i], starts[i + 1] - starts[i]), value)

    over_groups(
        count,
        lambda first, size: one_group(first, size, True),
        lambda first, size: one_group(first, size, False),
    )


def start_tiles(copies, count):
    def one_tile(tile, carry):
        for copy in copies(tile):
            copy.start()
        return carry

    lax.fori_loop(0, loaded_tiles(count), one_tile, 0)


def wait_tiles(copies, count):
    def one_tile(tile, carry):
        for copy in copies(tile):
            copy.wait()
        return carry

    lax.fori_loop(0, loaded_tiles(count), one_tile, 0)


def own_kernel(
    plan, table, times, gaps_occ, gaps_virt, occ, virt, polar,
    row_occ, row_virt, scaled, cols_occ, cols_virt, kept, row_sems, tile_sems, save_sems,
):
    which = plan.panels - 1
    slot = lax.div(lax.axis_index("ta"), jnp.int32(lax.axis_size("ta") // plan.blocks))
    own = table[plan.order + slot]
    count = table[which]
    place = pl.ds(pl.multiple_of(own * BLK, BLK), BLK)
    row_copies = (
        pltpu.make_async_copy(occ.at[place, :], row_occ, row_sems.at[0]),
        pltpu.make_async_copy(virt.at[place, :], row_virt, row_sems.at[1]),
    )
    copies = lambda tile: tile_copies(
        plan, table, which, tile, occ, virt, cols_occ, cols_virt, tile_sems
    )
    for copy in row_copies:
        copy.start()
    start_tiles(copies, count)
    for copy in row_copies:
        copy.wait()

    def scale(i, unrolled):
        scale_part(
            starts_of(scaled)[i] // BLK, times, gaps_occ, gaps_virt, row_occ, row_virt,
            scaled[i], unrolled,
        )

    starts = starts_of(scaled)

    def saved(first, size, i):
        part = (tile_range(first, size), pl.ds(starts[i], starts[i + 1] - starts[i]))
        return pltpu.make_async_copy(kept.at[part], polar.at[part], save_sems.at[first, i])

    def open_group(first, size):
        def take(i, part, value):
            kept[tile_range(first, size), part] = value
            saved(first, size, i).start()

        return take

    def finish(first, size):
        for i in range(len(scaled)):
            saved(first, size, i).wait()

    over_tiles(count, scale, copies, scaled, cols_occ, cols_virt, open_group)
    over_groups(count, finish, finish)


def rest_kernel(
    plan, table, times, cosine, gaps_occ, gaps_virt, other_rows, occ, virt, polar, probes,
    out, scaled, cols_occ, cols_virt, kept, fresh, terms,
    probe_two, probe_three, tile_sems, kept_sems,
):
    panels = plan.panels
    here = lax.axis_index("pa")
    rows = terms.shape[2]
    virt_count = virt.shape[1]

    def kept_copies(tile):
        place = tile_range(tile, 1)
        return (
            pltpu.make_async_copy(polar.at[place, :], kept.at[place, :], kept_sems.at[tile]),
        )

    def load_probes(which, first, size):
        held = probe_two if size == 2 else probe_three
        count = table[which]
        for tile in range(size):
            at = jnp.minimum(first + tile, jnp.maximum(count - 1, 0))
            value = probes[here * plan.blocks + table[plan.cols + which * plan.tiles + at]]
            held[:, tile * BLK : (tile + 1) * BLK] = jnp.where(
                first + tile < count, value, jnp.zeros_like(value)
            )
        return held

    terms[...] = jnp.zeros_like(terms)

    def apply(which, count, polars):
        def one_group(first, size):
            held = load_probes(which, first, size)
            terms[which] += jnp.dot(
                held[...], polars[tile_range(first, size), :], preferred_element_type=jnp.float32
            )

        over_groups(count, one_group, one_group)

    def one_other(which, carry):
        count = table[which]
        place = pl.ds(pl.multiple_of(which * BLK, BLK), BLK)
        row_virt = other_rows.at[place, pl.ds(0, virt_count)]
        row_occ = other_rows.at[place, pl.ds(virt_count, occ.shape[1])]
        copies = lambda tile: tile_copies(
            plan, table, which, tile, occ, virt, cols_occ, cols_virt, tile_sems
        )
        start_tiles(copies, count)

        @pl.when(which == 0)
        def _():
            start_tiles(kept_copies, table[panels - 1])

        def scale(i, unrolled):
            scale_part(
                starts_of(scaled)[i] // BLK, times, gaps_occ, gaps_virt, row_occ, row_virt,
                scaled[i], unrolled,
            )

        def open_group(first, size):
            def take(i, part, value):
                fresh[tile_range(first, size), part] = value

            return take

        over_tiles(count, scale, copies, scaled, cols_occ, cols_virt, open_group)
        apply(which, count, fresh)
        return carry

    lax.fori_loop(0, panels - 1, one_other, 0)
    wait_tiles(kept_copies, table[panels - 1])
    apply(panels - 1, table[panels - 1], kept)

    for which in range(panels):
        dest = lax.rem(here + which + 1, panels)

        def some_freqs(g, carry):
            totals = [jnp.zeros((NVEC, BLK), jnp.float32)] * FREQS
            for t in range(rows // BLK):
                value = terms[which, :, t * BLK : (t + 1) * BLK]
                for j in range(FREQS):
                    totals[j] += cosine[g * FREQS + j, t] * value
            for j in range(FREQS):
                out[(g * FREQS + j) * panels + dest] = totals[j]
            return carry

        lax.fori_loop(0, out.shape[0] // (panels * FREQS), some_freqs, 0)


def sum_kernel(plan, group, table, parts, out):
    panels, blocks = plan.panels, plan.blocks
    here = lax.axis_index("pa")
    for slot in range(blocks):
        total = jnp.zeros((NVEC, BLK), jnp.float32)
        for offset in range(1, panels):
            panel = lax.rem(here + offset, panels)
            for member in range(group):
                total += parts[(slot * group + member) * panels + panel]
        out[0, :, slot * BLK : (slot + 1) * BLK] = total
    for slot in range(blocks):
        total = parts[slot * group * panels + here]
        for member in range(1, group):
            total += parts[(slot * group + member) * panels + here]
        place = pl.ds(pl.multiple_of(table[plan.order + slot] * BLK, BLK), BLK)
        out[0, :, place] += total


def shards(
    occupied_orbitals, virtual_orbitals, occupied_gaps, virtual_gaps, tile_columns, probe_vectors
):
    count_ta = lax.axis_size("ta")
    panels = lax.axis_size("pa")
    panel_rows, occ_count = occupied_orbitals.shape
    virt_count = virtual_orbitals.shape[1]
    slice_width = probe_vectors.shape[1]
    tiles = tile_columns.shape[1]
    blocks = panel_rows // BLK
    group = count_ta // blocks
    local_times = NT // group
    rows = local_times * BLK
    if local_times % 8:
        parts_rows = (rows,)
    else:
        parts_rows = tuple(rows * part // 32 for part in (4, 8, 8, 12))
    plan = Plan(panels, tiles, blocks)
    width = min(slice_width, BLK)

    sent = pl.pallas_call(
        functools.partial(pack_kernel, group),
        in_specs=[ANY, ANY],
        out_specs=ANY,
        out_shape=jax.ShapeDtypeStruct((BLK, virt_count + occ_count), jnp.bfloat16),
        scratch_shapes=[pltpu.SemaphoreType.DMA((2,))],
        compiler_params=SMALL,
        name="pack",
    )(occupied_orbitals, virtual_orbitals)
    table, spread = pl.pallas_call(
        functools.partial(plan_kernel, plan, group),
        in_specs=[ANY, ANY, ANY],
        out_specs=(SMEM, VMEM),
        out_shape=(
            jax.ShapeDtypeStruct((plan.size,), jnp.int32),
            jax.ShapeDtypeStruct((count_ta, slice_width // width, NVEC, width), jnp.bfloat16),
        ),
        scratch_shapes=[
            pltpu.SMEM(tile_columns.shape, jnp.int32),
            pltpu.VMEM(probe_vectors.shape, jnp.bfloat16),
            pltpu.SMEM((2, blocks), jnp.int32),
            pltpu.SMEM((2, max(tiles, tiles * (panels - 1)) + 2), jnp.int32),
            pltpu.SMEM((2, blocks), jnp.int32),
            pltpu.SemaphoreType.DMA((2,)),
        ],
        compiler_params=SMALL,
        name="plan",
    )(tile_columns, probe_vectors, sent)

    others = [
        lax.ppermute(sent, "pa", [(q, (q - offset) % panels) for q in range(panels)])
        for offset in range(1, panels)
    ]
    other_rows = others[0] if panels == 2 else jnp.concatenate(others, axis=0)

    probes = lax.all_to_all(spread, "ta", 0, 0, tiled=True)
    if width < BLK:
        probes = probes.reshape(-1, BLK // width, NVEC, width).transpose(0, 2, 1, 3)
    probes = probes.reshape(-1, NVEC, BLK)

    times, cosine = quadrature_grids(NT, count_ta)
    if group > 1:
        first_time = (lax.axis_index("ta") % group) * local_times
        times = lax.dynamic_slice_in_dim(times, first_time, local_times, 0)
        cosine = lax.dynamic_slice_in_dim(cosine, first_time, local_times, 1)

    held_tiles = max(tiles, 2) * BLK
    scratch = [
        [
            (
                pltpu.VMEM((part, occ_count), jnp.bfloat16),
                pltpu.VMEM((part, virt_count), jnp.bfloat16),
            )
            for part in parts_rows
        ],
        pltpu.VMEM((held_tiles, occ_count), jnp.bfloat16),
        pltpu.VMEM((held_tiles, virt_count), jnp.bfloat16),
        pltpu.VMEM((held_tiles, rows), jnp.bfloat16),
    ]
    row_scratch = [
        pltpu.VMEM((BLK, occ_count), jnp.bfloat16),
        pltpu.VMEM((BLK, virt_count), jnp.bfloat16),
    ]
    tile_sems = pltpu.SemaphoreType.DMA((2, max(tiles, 2)))
    cost = pl.CostEstimate(
        flops=tiles * BLK * rows * (occ_count + virt_count), bytes_accessed=2**23, transcendentals=0
    )
    polar = pl.pallas_call(
        functools.partial(own_kernel, plan),
        in_specs=[SMEM, SMEM, VMEM, VMEM, ANY, ANY],
        out_specs=ANY,
        out_shape=jax.ShapeDtypeStruct((held_tiles, rows), jnp.bfloat16),
        scratch_shapes=row_scratch
        + scratch
        + [
            pltpu.SemaphoreType.DMA((2,)),
            tile_sems,
            pltpu.SemaphoreType.DMA((max(tiles, 2), len(parts_rows))),
        ],
        compiler_params=LARGE,
        cost_estimate=cost,
        name="own_tiles",
    )(table, times, occupied_gaps, virtual_gaps, occupied_orbitals, virtual_orbitals)

    partial_response = pl.pallas_call(
        functools.partial(rest_kernel, plan),
        in_specs=[SMEM, SMEM, SMEM, VMEM, VMEM, VMEM, ANY, ANY, ANY, VMEM],
        out_specs=VMEM,
        out_shape=jax.ShapeDtypeStruct((count_ta * panels, NVEC, BLK), jnp.float32),
        scratch_shapes=scratch
        + [
            pltpu.VMEM((held_tiles, rows), jnp.bfloat16),
            pltpu.VMEM((panels, NVEC, rows), jnp.float32),
            pltpu.VMEM((NVEC, 2 * BLK), jnp.bfloat16),
            pltpu.VMEM((NVEC, 3 * BLK), jnp.bfloat16),
        ]
        + [tile_sems, pltpu.SemaphoreType.DMA((max(tiles, 2),))],
        compiler_params=LARGE,
        cost_estimate=cost,
        name="other_tiles",
    )(
        table, times, cosine, occupied_gaps, virtual_gaps, other_rows,
        occupied_orbitals, virtual_orbitals, polar, probes,
    )

    parts = lax.all_to_all(partial_response, ("ta", "pa"), 0, 0, tiled=True)
    return pl.pallas_call(
        functools.partial(sum_kernel, plan, group),
        in_specs=[SMEM, VMEM],
        out_specs=VMEM,
        out_shape=jax.ShapeDtypeStruct((1, NVEC, panel_rows), jnp.float32),
        compiler_params=SMALL,
        name="sum_parts",
    )(table, parts)


def solution(mesh):
    placed = (P("pa", None), P("pa", None), P(), P(), P(), P(None, "ta"))
    return jax.shard_map(
        shards, mesh=mesh, in_specs=placed, out_specs=P("ta", None, "pa"), check_vma=False
    )
```

```python
import functools

import jax
import jax.numpy as jnp
from jax import lax
from jax.experimental import pallas as pl
from jax.experimental.pallas import tpu as pltpu
from jax.sharding import PartitionSpec as P

BLK = 128
NT = 32
NVEC = 32
FREQS = 4
LARGE = pltpu.CompilerParams(vmem_limit_bytes=52 * 2**20)
SMALL = pltpu.CompilerParams(vmem_limit_bytes=52 * 2**20)
NT_DIMS = (((1,), (1,)), ((), ()))
ANY = pl.BlockSpec(memory_space=pl.ANY)
SMEM = pl.BlockSpec(memory_space=pltpu.SMEM)
VMEM = pl.BlockSpec(memory_space=pltpu.VMEM)


def quadrature_grids(count_times, count_freqs):
    low_time = jnp.log(jnp.float32(0.05))
    high_time = jnp.log(jnp.float32(8.0))
    time_place = (jnp.arange(count_times, dtype=jnp.float32) + 0.5) / count_times
    times_grid = jnp.exp(low_time + (high_time - low_time) * time_place)
    weights_grid = times_grid * (high_time - low_time) / count_times
    low_freq = jnp.log(jnp.float32(0.05))
    high_freq = jnp.log(jnp.float32(20.0))
    freq_place = (jnp.arange(count_freqs, dtype=jnp.float32) + 0.5) / count_freqs
    freqs_grid = jnp.exp(low_freq + (high_freq - low_freq) * freq_place)
    cosine_table = 2.0 * weights_grid[None, :] * jnp.cos(freqs_grid[:, None] * times_grid[None, :])
    return (times_grid, cosine_table)


class Plan:
    def __init__(self, panels, tiles, blocks):
        self.panels = panels
        self.tiles = tiles
        self.blocks = blocks
        self.cols = panels
        self.order = panels + panels * tiles
        self.size = self.order + blocks


def pack_kernel(group, occ, virt, sent, sems):
    slot = lax.div(lax.axis_index("ta"), jnp.int32(group))
    virt_count = virt.shape[1]
    place = pl.ds(pl.multiple_of(slot * BLK, BLK), BLK)
    copies = (
        pltpu.make_async_copy(virt.at[place, :], sent.at[:, pl.ds(0, virt_count)], sems.at[0]),
        pltpu.make_async_copy(
            occ.at[place, :], sent.at[:, pl.ds(virt_count, occ.shape[1])], sems.at[1]
        ),
    )
    for copy in copies:
        copy.start()
    for copy in copies:
        copy.wait()


def plan_kernel(
    plan, group, tiles_hbm, probe_hbm, after, out, spread,
    listed, probe, keys, places, ranked, sems,
):
    panels, tiles, blocks = plan.panels, plan.tiles, plan.blocks
    here = lax.axis_index("pa")
    slot = lax.div(lax.axis_index("ta"), jnp.int32(group))
    copy_tiles = pltpu.make_async_copy(tiles_hbm, listed, sems.at[0])
    copy_probe = pltpu.make_async_copy(probe_hbm, probe, sems.at[1])
    copy_tiles.start()
    copy_probe.start()
    copy_tiles.wait()

    low = here * blocks

    def inside(row, k):
        column = listed[row, k]
        return ((column >= low) & (column < low + blocks)).astype(jnp.int32)

    def count(row):
        total = jnp.int32(0)
        for k in range(tiles):
            total += inside(row, k)
        return total

    most = max(tiles, tiles * (panels - 1))
    for kind in range(2):
        for value in range(most + 2):
            places[kind, value] = 0

    def one_count(s, carry):
        total = jnp.int32(0)
        for offset in range(1, panels):
            total += count(lax.rem(here + offset, panels) * blocks + s)
        for kind, value in enumerate((count(low + s), most - total)):
            keys[kind, s] = value
            places[kind, value + 1] = places[kind, value + 1] + 1
        return carry

    lax.fori_loop(0, blocks, one_count, 0)
    for kind in range(2):
        first = jnp.int32(0)
        for value in range(1, most + 2):
            first += places[kind, value]
            places[kind, value] = first

    def one_place(s, carry):
        for kind in range(2):
            value = keys[kind, s]
            rank = places[kind, value]
            places[kind, value] = rank + 1
            ranked[kind, rank] = s
        return carry

    lax.fori_loop(0, blocks, one_place, 0)
    for rank in range(blocks):
        out[plan.order + ranked[1, rank]] = ranked[0, rank]

    for which in range(panels):
        if which < panels - 1:
            row = lax.rem(here + which + 1, panels) * blocks + slot
        else:
            row = low + out[plan.order + slot]
        total = jnp.int32(0)
        for k in range(tiles):
            out[plan.cols + which * tiles + total] = listed[row, k] - low
            total += inside(row, k)
        out[which] = total

    copy_probe.wait()
    width = spread.shape[3]
    for piece in range(spread.shape[1]):
        value = probe[:, piece * width : (piece + 1) * width]
        for target in range(spread.shape[0]):
            spread[target, piece] = value


def scale_part(first_time, times, gaps_occ, gaps_virt, row_occ, row_virt, scaled, unrolled):
    def one_time(u, carry):
        place = pl.ds(u * BLK if unrolled else pl.multiple_of(u * BLK, BLK), BLK)
        minus_time = -times[first_time + u]
        for gaps, row, target in zip((gaps_occ, gaps_virt), (row_occ, row_virt), scaled):
            weights = jnp.exp(minus_time * gaps[...].reshape(1, -1))
            target[place, :] = (row[...].astype(jnp.float32) * weights).astype(jnp.bfloat16)
        return carry

    count = scaled[0].shape[0] // BLK
    if unrolled:
        for u in range(count):
            one_time(u, 0)
    else:
        lax.fori_loop(0, count, one_time, 0)


def starts_of(scaled):
    starts = [0]
    for part in scaled:
        starts.append(starts[-1] + part[0].shape[0])
    return starts


def loaded_tiles(count):
    return jnp.where(count == 1, 2, count)


def tile_copies(plan, table, which, tile, occ, virt, cols_occ, cols_virt, sems):
    last = jnp.maximum(table[which] - 1, 0)
    column = table[plan.cols + which * plan.tiles + jnp.minimum(tile, last)]
    source = pl.ds(pl.multiple_of(column * BLK, BLK), BLK)
    target = pl.ds(pl.multiple_of(tile * BLK, BLK), BLK)
    return (
        pltpu.make_async_copy(occ.at[source, :], cols_occ.at[target, :], sems.at[0, tile]),
        pltpu.make_async_copy(virt.at[source, :], cols_virt.at[target, :], sems.at[1, tile]),
    )


def over_groups(count, begin, later):
    triple = (lax.rem(count, 2) == 1) & (count >= 3)
    begun = jnp.where(triple, 3, 2)

    @pl.when(triple)
    def _():
        begin(0, 3)

    @pl.when((count > 0) & jnp.logical_not(triple))
    def _():
        begin(0, 2)

    def one_pair(g, carry):
        later(begun + 2 * g, 2)
        return carry

    lax.fori_loop(0, lax.div(loaded_tiles(count) - begun, 2), one_pair, 0)


def tile_range(first, size):
    if isinstance(first, int):
        return pl.ds(first * BLK, size * BLK)
    return pl.ds(pl.multiple_of(first * BLK, BLK), size * BLK)


def polar_part(columns, scaled, cols_occ, cols_virt):
    green_occ = lax.dot_general(
        cols_occ[columns, :], scaled[0][...], NT_DIMS, preferred_element_type=jnp.float32
    )
    green_virt = lax.dot_general(
        cols_virt[columns, :], scaled[1][...], NT_DIMS, preferred_element_type=jnp.float32
    )
    return (green_occ * green_virt).astype(jnp.bfloat16)


def over_tiles(count, scale, copies, scaled, cols_occ, cols_virt, open_group):
    starts = starts_of(scaled)

    def one_group(first, size, begins):
        if begins:
            scale(0, False)
        for tile in range(size):
            for copy in copies(first + tile):
                copy.wait()
        take = open_group(first, size)
        for i, part in enumerate(scaled):
            if begins and i + 1 < len(scaled):
                scale(i + 1, True)
            value = polar_part(tile_range(first, size), part, cols_occ, cols_virt)
            take(i, pl.ds(starts[i], starts[i + 1] - starts[i]), value)

    over_groups(
        count,
        lambda first, size: one_group(first, size, True),
        lambda first, size: one_group(first, size, False),
    )


def start_tiles(copies, count):
    def one_tile(tile, carry):
        for copy in copies(tile):
            copy.start()
        return carry

    lax.fori_loop(0, loaded_tiles(count), one_tile, 0)


def wait_tiles(copies, count):
    def one_tile(tile, carry):
        for copy in copies(tile):
            copy.wait()
        return carry

    lax.fori_loop(0, loaded_tiles(count), one_tile, 0)


def own_kernel(
    plan, table, times, gaps_occ, gaps_virt, occ, virt, polar,
    row_occ, row_virt, scaled, cols_occ, cols_virt, kept, row_sems, tile_sems, save_sems,
):
    which = plan.panels - 1
    slot = lax.div(lax.axis_index("ta"), jnp.int32(lax.axis_size("ta") // plan.blocks))
    own = table[plan.order + slot]
    count = table[which]
    place = pl.ds(pl.multiple_of(own * BLK, BLK), BLK)
    row_copies = (
        pltpu.make_async_copy(occ.at[place, :], row_occ, row_sems.at[0]),
        pltpu.make_async_copy(virt.at[place, :], row_virt, row_sems.at[1]),
    )
    copies = lambda tile: tile_copies(
        plan, table, which, tile, occ, virt, cols_occ, cols_virt, tile_sems
    )
    for copy in row_copies:
        copy.start()
    start_tiles(copies, count)
    for copy in row_copies:
        copy.wait()

    def scale(i, unrolled):
        scale_part(
            starts_of(scaled)[i] // BLK, times, gaps_occ, gaps_virt, row_occ, row_virt,
            scaled[i], unrolled,
        )

    starts = starts_of(scaled)

    def saved(first, size, i):
        part = (tile_range(first, size), pl.ds(starts[i], starts[i + 1] - starts[i]))
        return pltpu.make_async_copy(kept.at[part], polar.at[part], save_sems.at[first, i])

    def open_group(first, size):
        def take(i, part, value):
            kept[tile_range(first, size), part] = value
            saved(first, size, i).start()

        return take

    def finish(first, size):
        for i in range(len(scaled)):
            saved(first, size, i).wait()

    over_tiles(count, scale, copies, scaled, cols_occ, cols_virt, open_group)
    over_groups(count, finish, finish)


def rest_kernel(
    plan, table, times, cosine, gaps_occ, gaps_virt, other_rows, occ, virt, polar, probes,
    out, scaled, cols_occ, cols_virt, kept, fresh, terms,
    probe_two, probe_three, tile_sems, kept_sems,
):
    panels = plan.panels
    here = lax.axis_index("pa")
    rows = terms.shape[2]
    virt_count = virt.shape[1]

    def kept_copies(tile):
        place = tile_range(tile, 1)
        return (
            pltpu.make_async_copy(polar.at[place, :], kept.at[place, :], kept_sems.at[tile]),
        )

    def load_probes(which, first, size):
        held = probe_two if size == 2 else probe_three
        count = table[which]
        for tile in range(size):
            at = jnp.minimum(first + tile, jnp.maximum(count - 1, 0))
            value = probes[here * plan.blocks + table[plan.cols + which * plan.tiles + at]]
            held[:, tile * BLK : (tile + 1) * BLK] = jnp.where(
                first + tile < count, value, jnp.zeros_like(value)
            )
        return held

    terms[...] = jnp.zeros_like(terms)

    def apply(which, count, polars):
        def one_group(first, size):
            held = load_probes(which, first, size)
            terms[which] += jnp.dot(
                held[...], polars[tile_range(first, size), :], preferred_element_type=jnp.float32
            )

        over_groups(count, one_group, one_group)

    def one_other(which, carry):
        count = table[which]
        place = pl.ds(pl.multiple_of(which * BLK, BLK), BLK)
        row_virt = other_rows.at[place, pl.ds(0, virt_count)]
        row_occ = other_rows.at[place, pl.ds(virt_count, occ.shape[1])]
        copies = lambda tile: tile_copies(
            plan, table, which, tile, occ, virt, cols_occ, cols_virt, tile_sems
        )
        start_tiles(copies, count)

        @pl.when(which == 0)
        def _():
            start_tiles(kept_copies, table[panels - 1])

        def scale(i, unrolled):
            scale_part(
                starts_of(scaled)[i] // BLK, times, gaps_occ, gaps_virt, row_occ, row_virt,
                scaled[i], unrolled,
            )

        def open_group(first, size):
            def take(i, part, value):
                fresh[tile_range(first, size), part] = value

            return take

        over_tiles(count, scale, copies, scaled, cols_occ, cols_virt, open_group)
        apply(which, count, fresh)
        return carry

    lax.fori_loop(0, panels - 1, one_other, 0)
    wait_tiles(kept_copies, table[panels - 1])
    apply(panels - 1, table[panels - 1], kept)

    for which in range(panels):
        dest = lax.rem(here + which + 1, panels)

        def some_freqs(g, carry):
            totals = [jnp.zeros((NVEC, BLK), jnp.float32)] * FREQS
            for t in range(rows // BLK):
                value = terms[which, :, t * BLK : (t + 1) * BLK]
                for j in range(FREQS):
                    totals[j] += cosine[g * FREQS + j, t] * value
            for j in range(FREQS):
                out[(g * FREQS + j) * panels + dest] = totals[j]
            return carry

        lax.fori_loop(0, out.shape[0] // (panels * FREQS), some_freqs, 0)


def sum_kernel(plan, group, table, parts, out):
    panels, blocks = plan.panels, plan.blocks
    here = lax.axis_index("pa")
    for slot in range(blocks):
        total = jnp.zeros((NVEC, BLK), jnp.float32)
        for offset in range(1, panels):
            panel = lax.rem(here + offset, panels)
            for member in range(group):
                total += parts[(slot * group + member) * panels + panel]
        out[0, :, slot * BLK : (slot + 1) * BLK] = total
    for slot in range(blocks):
        total = parts[slot * group * panels + here]
        for member in range(1, group):
            total += parts[(slot * group + member) * panels + here]
        place = pl.ds(pl.multiple_of(table[plan.order + slot] * BLK, BLK), BLK)
        out[0, :, place] += total


def shards(
    occupied_orbitals, virtual_orbitals, occupied_gaps, virtual_gaps, tile_columns, probe_vectors
):
    count_ta = lax.axis_size("ta")
    panels = lax.axis_size("pa")
    panel_rows, occ_count = occupied_orbitals.shape
    virt_count = virtual_orbitals.shape[1]
    slice_width = probe_vectors.shape[1]
    tiles = tile_columns.shape[1]
    blocks = panel_rows // BLK
    group = count_ta // blocks
    local_times = NT // group
    rows = local_times * BLK
    if local_times % 8:
        parts_rows = (rows,)
    else:
        parts_rows = tuple(rows * part // 32 for part in (4, 8, 8, 12))
    plan = Plan(panels, tiles, blocks)
    width = min(slice_width, BLK)

    sent = pl.pallas_call(
        functools.partial(pack_kernel, group),
        in_specs=[ANY, ANY],
        out_specs=ANY,
        out_shape=jax.ShapeDtypeStruct((BLK, virt_count + occ_count), jnp.bfloat16),
        scratch_shapes=[pltpu.SemaphoreType.DMA((2,))],
        compiler_params=SMALL,
        name="pack",
    )(occupied_orbitals, virtual_orbitals)
    table, spread = pl.pallas_call(
        functools.partial(plan_kernel, plan, group),
        in_specs=[ANY, ANY, ANY],
        out_specs=(SMEM, VMEM),
        out_shape=(
            jax.ShapeDtypeStruct((plan.size,), jnp.int32),
            jax.ShapeDtypeStruct((count_ta, slice_width // width, NVEC, width), jnp.bfloat16),
        ),
        scratch_shapes=[
            pltpu.SMEM(tile_columns.shape, jnp.int32),
            pltpu.VMEM(probe_vectors.shape, jnp.bfloat16),
            pltpu.SMEM((2, blocks), jnp.int32),
            pltpu.SMEM((2, max(tiles, tiles * (panels - 1)) + 2), jnp.int32),
            pltpu.SMEM((2, blocks), jnp.int32),
            pltpu.SemaphoreType.DMA((2,)),
        ],
        compiler_params=SMALL,
        name="plan",
    )(tile_columns, probe_vectors, sent)

    others = [
        lax.ppermute(sent, "pa", [(q, (q - offset) % panels) for q in range(panels)])
        for offset in range(1, panels)
    ]
    other_rows = others[0] if panels == 2 else jnp.concatenate(others, axis=0)

    probes = lax.all_to_all(spread, "ta", 0, 0, tiled=True)
    if width < BLK:
        probes = probes.reshape(-1, BLK // width, NVEC, width).transpose(0, 2, 1, 3)
    probes = probes.reshape(-1, NVEC, BLK)

    times, cosine = quadrature_grids(NT, count_ta)
    if group > 1:
        first_time = (lax.axis_index("ta") % group) * local_times
        times = lax.dynamic_slice_in_dim(times, first_time, local_times, 0)
        cosine = lax.dynamic_slice_in_dim(cosine, first_time, local_times, 1)

    held_tiles = max(tiles, 2) * BLK
    scratch = [
        [
            (
                pltpu.VMEM((part, occ_count), jnp.bfloat16),
                pltpu.VMEM((part, virt_count), jnp.bfloat16),
            )
            for part in parts_rows
        ],
        pltpu.VMEM((held_tiles, occ_count), jnp.bfloat16),
        pltpu.VMEM((held_tiles, virt_count), jnp.bfloat16),
        pltpu.VMEM((held_tiles, rows), jnp.bfloat16),
    ]
    row_scratch = [
        pltpu.VMEM((BLK, occ_count), jnp.bfloat16),
        pltpu.VMEM((BLK, virt_count), jnp.bfloat16),
    ]
    tile_sems = pltpu.SemaphoreType.DMA((2, max(tiles, 2)))
    cost = pl.CostEstimate(
        flops=tiles * BLK * rows * (occ_count + virt_count), bytes_accessed=2**23, transcendentals=0
    )
    polar = pl.pallas_call(
        functools.partial(own_kernel, plan),
        in_specs=[SMEM, SMEM, VMEM, VMEM, ANY, ANY],
        out_specs=ANY,
        out_shape=jax.ShapeDtypeStruct((held_tiles, rows), jnp.bfloat16),
        scratch_shapes=row_scratch
        + scratch
        + [
            pltpu.SemaphoreType.DMA((2,)),
            tile_sems,
            pltpu.SemaphoreType.DMA((max(tiles, 2), len(parts_rows))),
        ],
        compiler_params=LARGE,
        cost_estimate=cost,
        name="own_tiles",
    )(table, times, occupied_gaps, virtual_gaps, occupied_orbitals, virtual_orbitals)

    partial_response = pl.pallas_call(
        functools.partial(rest_kernel, plan),
        in_specs=[SMEM, SMEM, SMEM, VMEM, VMEM, VMEM, ANY, ANY, ANY, VMEM],
        out_specs=VMEM,
        out_shape=jax.ShapeDtypeStruct((count_ta * panels, NVEC, BLK), jnp.float32),
        scratch_shapes=scratch
        + [
            pltpu.VMEM((held_tiles, rows), jnp.bfloat16),
            pltpu.VMEM((panels, NVEC, rows), jnp.float32),
            pltpu.VMEM((NVEC, 2 * BLK), jnp.bfloat16),
            pltpu.VMEM((NVEC, 3 * BLK), jnp.bfloat16),
        ]
        + [tile_sems, pltpu.SemaphoreType.DMA((max(tiles, 2),))],
        compiler_params=LARGE,
        cost_estimate=cost,
        name="other_tiles",
    )(
        table, times, cosine, occupied_gaps, virtual_gaps, other_rows,
        occupied_orbitals, virtual_orbitals, polar, probes,
    )

    parts = lax.all_to_all(partial_response, ("ta", "pa"), 0, 0, tiled=True)
    return pl.pallas_call(
        functools.partial(sum_kernel, plan, group),
        in_specs=[SMEM, VMEM],
        out_specs=VMEM,
        out_shape=jax.ShapeDtypeStruct((1, NVEC, panel_rows), jnp.float32),
        compiler_params=SMALL,
        name="sum_parts",
    )(table, parts)


def solution(mesh):
    placed = (P("pa", None), P("pa", None), P(), P(), P(), P(None, "ta"))
    return jax.shard_map(
        shards, mesh=mesh, in_specs=placed, out_specs=P("ta", None, "pa"), check_vma=False
    )
```

```python
import functools

import jax
import jax.numpy as jnp
from jax import lax
from jax.experimental import pallas as pl
from jax.experimental.pallas import tpu as pltpu
from jax.sharding import PartitionSpec as P

BLK = 128
NT = 32
NVEC = 32
FREQS = 4
LARGE = pltpu.CompilerParams(vmem_limit_bytes=52 * 2**20)
SMALL = pltpu.CompilerParams(vmem_limit_bytes=52 * 2**20)
NT_DIMS = (((1,), (1,)), ((), ()))
ANY = pl.BlockSpec(memory_space=pl.ANY)
SMEM = pl.BlockSpec(memory_space=pltpu.SMEM)
VMEM = pl.BlockSpec(memory_space=pltpu.VMEM)


def quadrature_grids(count_times, count_freqs):
    low_time = jnp.log(jnp.float32(0.05))
    high_time = jnp.log(jnp.float32(8.0))
    time_place = (jnp.arange(count_times, dtype=jnp.float32) + 0.5) / count_times
    times_grid = jnp.exp(low_time + (high_time - low_time) * time_place)
    weights_grid = times_grid * (high_time - low_time) / count_times
    low_freq = jnp.log(jnp.float32(0.05))
    high_freq = jnp.log(jnp.float32(20.0))
    freq_place = (jnp.arange(count_freqs, dtype=jnp.float32) + 0.5) / count_freqs
    freqs_grid = jnp.exp(low_freq + (high_freq - low_freq) * freq_place)
    cosine_table = 2.0 * weights_grid[None, :] * jnp.cos(freqs_grid[:, None] * times_grid[None, :])
    return (times_grid, cosine_table)


class Plan:
    def __init__(self, panels, tiles, blocks):
        self.panels = panels
        self.tiles = tiles
        self.blocks = blocks
        self.cols = panels
        self.order = panels + panels * tiles
        self.slots = self.order + blocks
        self.size = self.slots + blocks


def pack_kernel(group, occ, virt, sent, sems):
    slot = lax.div(lax.axis_index("ta"), jnp.int32(group))
    virt_count = virt.shape[1]
    place = pl.ds(pl.multiple_of(slot * BLK, BLK), BLK)
    copies = (
        pltpu.make_async_copy(virt.at[place, :], sent.at[:, pl.ds(0, virt_count)], sems.at[0]),
        pltpu.make_async_copy(
            occ.at[place, :], sent.at[:, pl.ds(virt_count, occ.shape[1])], sems.at[1]
        ),
    )
    for copy in copies:
        copy.start()
    for copy in copies:
        copy.wait()


def plan_kernel(
    plan, group, tiles_hbm, probe_hbm, after, out, spread,
    listed, probe, keys, places, ranked, sems,
):
    panels, tiles, blocks = plan.panels, plan.tiles, plan.blocks
    here = lax.axis_index("pa")
    slot = lax.div(lax.axis_index("ta"), jnp.int32(group))
    copy_tiles = pltpu.make_async_copy(tiles_hbm, listed, sems.at[0])
    copy_probe = pltpu.make_async_copy(probe_hbm, probe, sems.at[1])
    copy_tiles.start()
    copy_probe.start()
    copy_tiles.wait()

    low = here * blocks

    def inside(row, k):
        column = listed[row, k]
        return ((column >= low) & (column < low + blocks)).astype(jnp.int32)

    def count(row):
        total = jnp.int32(0)
        for k in range(tiles):
            total += inside(row, k)
        return total

    most = max(tiles, tiles * (panels - 1))
    for kind in range(2):
        for value in range(most + 2):
            places[kind, value] = 0

    def one_count(s, carry):
        total = jnp.int32(0)
        for offset in range(1, panels):
            total += count(lax.rem(here + offset, panels) * blocks + s)
        for kind, value in enumerate((count(low + s), most - total)):
            keys[kind, s] = value
            places[kind, value + 1] = places[kind, value + 1] + 1
        return carry

    lax.fori_loop(0, blocks, one_count, 0)
    for kind in range(2):
        first = jnp.int32(0)
        for value in range(1, most + 2):
            first += places[kind, value]
            places[kind, value] = first

    def one_place(s, carry):
        for kind in range(2):
            value = keys[kind, s]
            rank = places[kind, value]
            places[kind, value] = rank + 1
            ranked[kind, rank] = s
        return carry

    lax.fori_loop(0, blocks, one_place, 0)
    for rank in range(blocks):
        out[plan.order + ranked[1, rank]] = ranked[0, rank]
        out[plan.slots + ranked[0, rank]] = ranked[1, rank]

    for which in range(panels):
        if which < panels - 1:
            row = lax.rem(here + which + 1, panels) * blocks + slot
        else:
            row = low + out[plan.order + slot]
        total = jnp.int32(0)
        for k in range(tiles):
            out[plan.cols + which * tiles + total] = listed[row, k] - low
            total += inside(row, k)
        out[which] = total

    copy_probe.wait()
    width = spread.shape[3]
    for piece in range(spread.shape[1]):
        value = probe[:, piece * width : (piece + 1) * width]
        for target in range(spread.shape[0]):
            spread[target, piece] = value


def scale_part(first_time, times, gaps_occ, gaps_virt, row_occ, row_virt, scaled, unrolled):
    def one_time(u, carry):
        place = pl.ds(u * BLK if unrolled else pl.multiple_of(u * BLK, BLK), BLK)
        minus_time = -times[first_time + u]
        for gaps, row, target in zip((gaps_occ, gaps_virt), (row_occ, row_virt), scaled):
            weights = jnp.exp(minus_time * gaps[...].reshape(1, -1))
            target[place, :] = (row[...].astype(jnp.float32) * weights).astype(jnp.bfloat16)
        return carry

    count = scaled[0].shape[0] // BLK
    if unrolled:
        for u in range(count):
            one_time(u, 0)
    else:
        lax.fori_loop(0, count, one_time, 0)


def starts_of(scaled):
    starts = [0]
    for part in scaled:
        starts.append(starts[-1] + part[0].shape[0])
    return starts


def loaded_tiles(count):
    return jnp.where(count == 1, 2, count)


def tile_copies(plan, table, which, tile, occ, virt, cols_occ, cols_virt, sems):
    last = jnp.maximum(table[which] - 1, 0)
    column = table[plan.cols + which * plan.tiles + jnp.minimum(tile, last)]
    source = pl.ds(pl.multiple_of(column * BLK, BLK), BLK)
    target = pl.ds(pl.multiple_of(tile * BLK, BLK), BLK)
    return (
        pltpu.make_async_copy(occ.at[source, :], cols_occ.at[target, :], sems.at[0, tile]),
        pltpu.make_async_copy(virt.at[source, :], cols_virt.at[target, :], sems.at[1, tile]),
    )


def over_groups(count, begin, later):
    triple = (lax.rem(count, 2) == 1) & (count >= 3)
    begun = jnp.where(triple, 3, 2)

    @pl.when(triple)
    def _():
        begin(0, 3)

    @pl.when((count > 0) & jnp.logical_not(triple))
    def _():
        begin(0, 2)

    def one_pair(g, carry):
        later(begun + 2 * g, 2)
        return carry

    lax.fori_loop(0, lax.div(loaded_tiles(count) - begun, 2), one_pair, 0)


def tile_range(first, size):
    if isinstance(first, int):
        return pl.ds(first * BLK, size * BLK)
    return pl.ds(pl.multiple_of(first * BLK, BLK), size * BLK)


def polar_part(columns, scaled, cols_occ, cols_virt):
    green_occ = lax.dot_general(
        cols_occ[columns, :], scaled[0][...], NT_DIMS, preferred_element_type=jnp.float32
    )
    green_virt = lax.dot_general(
        cols_virt[columns, :], scaled[1][...], NT_DIMS, preferred_element_type=jnp.float32
    )
    return (green_occ * green_virt).astype(jnp.bfloat16)


def over_tiles(count, scale, copies, scaled, cols_occ, cols_virt, open_group):
    starts = starts_of(scaled)

    def one_group(first, size, begins):
        if begins:
            scale(0, False)
        for tile in range(size):
            for copy in copies(first + tile):
                copy.wait()
        take = open_group(first, size)
        for i, part in enumerate(scaled):
            if begins and i + 1 < len(scaled):
                scale(i + 1, True)
            value = polar_part(tile_range(first, size), part, cols_occ, cols_virt)
            take(i, pl.ds(starts[i], starts[i + 1] - starts[i]), value)

    over_groups(
        count,
        lambda first, size: one_group(first, size, True),
        lambda first, size: one_group(first, size, False),
    )


def start_tiles(copies, count):
    def one_tile(tile, carry):
        for copy in copies(tile):
            copy.start()
        return carry

    lax.fori_loop(0, loaded_tiles(count), one_tile, 0)


def wait_tiles(copies, count):
    def one_tile(tile, carry):
        for copy in copies(tile):
            copy.wait()
        return carry

    lax.fori_loop(0, loaded_tiles(count), one_tile, 0)


def own_kernel(
    plan, table, times, gaps_occ, gaps_virt, occ, virt, polar,
    row_occ, row_virt, scaled, cols_occ, cols_virt, kept, row_sems, tile_sems, save_sems,
):
    which = plan.panels - 1
    slot = lax.div(lax.axis_index("ta"), jnp.int32(lax.axis_size("ta") // plan.blocks))
    own = table[plan.order + slot]
    count = table[which]
    place = pl.ds(pl.multiple_of(own * BLK, BLK), BLK)
    row_copies = (
        pltpu.make_async_copy(occ.at[place, :], row_occ, row_sems.at[0]),
        pltpu.make_async_copy(virt.at[place, :], row_virt, row_sems.at[1]),
    )
    copies = lambda tile: tile_copies(
        plan, table, which, tile, occ, virt, cols_occ, cols_virt, tile_sems
    )
    for copy in row_copies:
        copy.start()
    start_tiles(copies, count)
    for copy in row_copies:
        copy.wait()

    def scale(i, unrolled):
        scale_part(
            starts_of(scaled)[i] // BLK, times, gaps_occ, gaps_virt, row_occ, row_virt,
            scaled[i], unrolled,
        )

    starts = starts_of(scaled)

    def saved(first, size, i):
        part = (tile_range(first, size), pl.ds(starts[i], starts[i + 1] - starts[i]))
        return pltpu.make_async_copy(kept.at[part], polar.at[part], save_sems.at[first, i])

    def open_group(first, size):
        def take(i, part, value):
            kept[tile_range(first, size), part] = value
            saved(first, size, i).start()

        return take

    def finish(first, size):
        for i in range(len(scaled)):
            saved(first, size, i).wait()

    over_tiles(count, scale, copies, scaled, cols_occ, cols_virt, open_group)
    over_groups(count, finish, finish)


def rest_kernel(
    plan, table, times, cosine, gaps_occ, gaps_virt, other_rows, occ, virt, polar, probes,
    out, scaled, cols_occ, cols_virt, kept, fresh, terms,
    probe_two, probe_three, tile_sems, kept_sems,
):
    panels = plan.panels
    here = lax.axis_index("pa")
    rows = terms.shape[2]
    virt_count = virt.shape[1]

    def kept_copies(tile):
        place = tile_range(tile, 1)
        return (
            pltpu.make_async_copy(polar.at[place, :], kept.at[place, :], kept_sems.at[tile]),
        )

    def load_probes(which, first, size):
        held = probe_two if size == 2 else probe_three
        count = table[which]
        for tile in range(size):
            at = jnp.minimum(first + tile, jnp.maximum(count - 1, 0))
            value = probes[here * plan.blocks + table[plan.cols + which * plan.tiles + at]]
            held[:, tile * BLK : (tile + 1) * BLK] = jnp.where(
                first + tile < count, value, jnp.zeros_like(value)
            )
        return held

    terms[...] = jnp.zeros_like(terms)

    def apply(which, count, polars):
        def one_group(first, size):
            held = load_probes(which, first, size)
            terms[which] += jnp.dot(
                held[...], polars[tile_range(first, size), :], preferred_element_type=jnp.float32
            )

        over_groups(count, one_group, one_group)

    def one_other(which, carry):
        count = table[which]
        place = pl.ds(pl.multiple_of(which * BLK, BLK), BLK)
        row_virt = other_rows.at[place, pl.ds(0, virt_count)]
        row_occ = other_rows.at[place, pl.ds(virt_count, occ.shape[1])]
        copies = lambda tile: tile_copies(
            plan, table, which, tile, occ, virt, cols_occ, cols_virt, tile_sems
        )
        start_tiles(copies, count)

        @pl.when(which == 0)
        def _():
            start_tiles(kept_copies, table[panels - 1])

        def scale(i, unrolled):
            scale_part(
                starts_of(scaled)[i] // BLK, times, gaps_occ, gaps_virt, row_occ, row_virt,
                scaled[i], unrolled,
            )

        def open_group(first, size):
            def take(i, part, value):
                fresh[tile_range(first, size), part] = value

            return take

        over_tiles(count, scale, copies, scaled, cols_occ, cols_virt, open_group)
        apply(which, count, fresh)
        return carry

    lax.fori_loop(0, panels - 1, one_other, 0)
    wait_tiles(kept_copies, table[panels - 1])
    apply(panels - 1, table[panels - 1], kept)

    for which in range(panels):
        dest = lax.rem(here + which + 1, panels)

        def some_freqs(g, carry):
            totals = [jnp.zeros((NVEC, BLK), jnp.float32)] * FREQS
            for t in range(rows // BLK):
                value = terms[which, :, t * BLK : (t + 1) * BLK]
                for j in range(FREQS):
                    totals[j] += cosine[g * FREQS + j, t] * value
            for j in range(FREQS):
                out[(g * FREQS + j) * panels + dest] = totals[j]
            return carry

        lax.fori_loop(0, out.shape[0] // (panels * FREQS), some_freqs, 0)


def sum_kernel(plan, group, table, parts, out, total, sems):
    panels, blocks = plan.panels, plan.blocks
    here = lax.axis_index("pa")
    piece = blocks // sems.shape[0]
    copies = []
    for block in range(blocks):
        own = table[plan.slots + block] * (group * panels) + here
        value = parts[own]
        for member in range(1, group):
            value += parts[own + member * panels]
        for offset in range(1, panels):
            panel = lax.rem(here + offset, panels)
            for member in range(group):
                value += parts[(block * group + member) * panels + panel]
        total[0, :, block * BLK : (block + 1) * BLK] = value
        if (block + 1) % piece == 0:
            columns = pl.ds((block + 1 - piece) * BLK, piece * BLK)
            copies.append(
                pltpu.make_async_copy(
                    total.at[:, :, columns], out.at[:, :, columns], sems.at[block // piece]
                )
            )
            copies[-1].start()
    for copy in copies:
        copy.wait()


def shards(
    occupied_orbitals, virtual_orbitals, occupied_gaps, virtual_gaps, tile_columns, probe_vectors
):
    count_ta = lax.axis_size("ta")
    panels = lax.axis_size("pa")
    panel_rows, occ_count = occupied_orbitals.shape
    virt_count = virtual_orbitals.shape[1]
    slice_width = probe_vectors.shape[1]
    tiles = tile_columns.shape[1]
    blocks = panel_rows // BLK
    group = count_ta // blocks
    local_times = NT // group
    rows = local_times * BLK
    if local_times % 8:
        parts_rows = (rows,)
    else:
        parts_rows = tuple(rows * part // 32 for part in (4, 8, 8, 12))
    plan = Plan(panels, tiles, blocks)
    width = min(slice_width, BLK)

    sent = pl.pallas_call(
        functools.partial(pack_kernel, group),
        in_specs=[ANY, ANY],
        out_specs=ANY,
        out_shape=jax.ShapeDtypeStruct((BLK, virt_count + occ_count), jnp.bfloat16),
        scratch_shapes=[pltpu.SemaphoreType.DMA((2,))],
        compiler_params=SMALL,
        name="pack",
    )(occupied_orbitals, virtual_orbitals)
    table, spread = pl.pallas_call(
        functools.partial(plan_kernel, plan, group),
        in_specs=[ANY, ANY, ANY],
        out_specs=(SMEM, VMEM),
        out_shape=(
            jax.ShapeDtypeStruct((plan.size,), jnp.int32),
            jax.ShapeDtypeStruct((count_ta, slice_width // width, NVEC, width), jnp.bfloat16),
        ),
        scratch_shapes=[
            pltpu.SMEM(tile_columns.shape, jnp.int32),
            pltpu.VMEM(probe_vectors.shape, jnp.bfloat16),
            pltpu.SMEM((2, blocks), jnp.int32),
            pltpu.SMEM((2, max(tiles, tiles * (panels - 1)) + 2), jnp.int32),
            pltpu.SMEM((2, blocks), jnp.int32),
            pltpu.SemaphoreType.DMA((2,)),
        ],
        compiler_params=SMALL,
        name="plan",
    )(tile_columns, probe_vectors, sent)

    others = [
        lax.ppermute(sent, "pa", [(q, (q - offset) % panels) for q in range(panels)])
        for offset in range(1, panels)
    ]
    other_rows = others[0] if panels == 2 else jnp.concatenate(others, axis=0)

    probes = lax.all_to_all(spread, "ta", 0, 0, tiled=True)
    if width < BLK:
        probes = probes.reshape(-1, BLK // width, NVEC, width).transpose(0, 2, 1, 3)
    probes = probes.reshape(-1, NVEC, BLK)

    times, cosine = quadrature_grids(NT, count_ta)
    if group > 1:
        first_time = (lax.axis_index("ta") % group) * local_times
        times = lax.dynamic_slice_in_dim(times, first_time, local_times, 0)
        cosine = lax.dynamic_slice_in_dim(cosine, first_time, local_times, 1)

    held_tiles = max(tiles, 2) * BLK
    scratch = [
        [
            (
                pltpu.VMEM((part, occ_count), jnp.bfloat16),
                pltpu.VMEM((part, virt_count), jnp.bfloat16),
            )
            for part in parts_rows
        ],
        pltpu.VMEM((held_tiles, occ_count), jnp.bfloat16),
        pltpu.VMEM((held_tiles, virt_count), jnp.bfloat16),
        pltpu.VMEM((held_tiles, rows), jnp.bfloat16),
    ]
    row_scratch = [
        pltpu.VMEM((BLK, occ_count), jnp.bfloat16),
        pltpu.VMEM((BLK, virt_count), jnp.bfloat16),
    ]
    tile_sems = pltpu.SemaphoreType.DMA((2, max(tiles, 2)))
    cost = pl.CostEstimate(
        flops=tiles * BLK * rows * (occ_count + virt_count), bytes_accessed=2**23, transcendentals=0
    )
    polar = pl.pallas_call(
        functools.partial(own_kernel, plan),
        in_specs=[SMEM, SMEM, VMEM, VMEM, ANY, ANY],
        out_specs=ANY,
        out_shape=jax.ShapeDtypeStruct((held_tiles, rows), jnp.bfloat16),
        scratch_shapes=row_scratch
        + scratch
        + [
            pltpu.SemaphoreType.DMA((2,)),
            tile_sems,
            pltpu.SemaphoreType.DMA((max(tiles, 2), len(parts_rows))),
        ],
        compiler_params=LARGE,
        cost_estimate=cost,
        name="own_tiles",
    )(table, times, occupied_gaps, virtual_gaps, occupied_orbitals, virtual_orbitals)

    partial_response = pl.pallas_call(
        functools.partial(rest_kernel, plan),
        in_specs=[SMEM, SMEM, SMEM, VMEM, VMEM, VMEM, ANY, ANY, ANY, VMEM],
        out_specs=VMEM,
        out_shape=jax.ShapeDtypeStruct((count_ta * panels, NVEC, BLK), jnp.float32),
        scratch_shapes=scratch
        + [
            pltpu.VMEM((held_tiles, rows), jnp.bfloat16),
            pltpu.VMEM((panels, NVEC, rows), jnp.float32),
            pltpu.VMEM((NVEC, 2 * BLK), jnp.bfloat16),
            pltpu.VMEM((NVEC, 3 * BLK), jnp.bfloat16),
        ]
        + [tile_sems, pltpu.SemaphoreType.DMA((max(tiles, 2),))],
        compiler_params=LARGE,
        cost_estimate=cost,
        name="other_tiles",
    )(
        table, times, cosine, occupied_gaps, virtual_gaps, other_rows,
        occupied_orbitals, virtual_orbitals, polar, probes,
    )

    parts = lax.all_to_all(partial_response, ("ta", "pa"), 0, 0, tiled=True)
    return pl.pallas_call(
        functools.partial(sum_kernel, plan, group),
        in_specs=[SMEM, VMEM],
        out_specs=ANY,
        out_shape=jax.ShapeDtypeStruct((1, NVEC, panel_rows), jnp.float32),
        scratch_shapes=[
            pltpu.VMEM((1, NVEC, panel_rows), jnp.float32),
            pltpu.SemaphoreType.DMA((4,)),
        ],
        compiler_params=SMALL,
        name="sum_parts",
    )(table, parts)


def solution(mesh):
    placed = (P("pa", None), P("pa", None), P(), P(), P(), P(None, "ta"))
    return jax.shard_map(
        shards, mesh=mesh, in_specs=placed, out_specs=P("ta", None, "pa"), check_vma=False
    )
```
